32 devices in a mesh: groups: 2 (over y), section: 4 (over z), tensor: 4 (over x, core).
Axes of the slice: x: 2, y: 2, z: 4, core: 2. Of those that a mesh axis runs over, the one named last changes fastest.
Arguments:
- hidden: bfloat16 [128, 32, 8192], P(('groups', 'section'), None, 'tensor'), parts along dimension 0, may hold values from -6 to 6
- kv_weight: bfloat16 [8192, 2, 1024], P(None, None, 'tensor'), may hold values from -0.0625 to 0.0625
- kv_bias: bfloat16 [2, 1024], P(None, 'tensor'), may hold values from -3 to 3
- prompt_len: int32 [128], P('groups'), parts along dimension 0, may hold values from 1 to 32, as said below
- owner: int32 [128], P('groups'), parts along dimension 0, may hold values from 0 to 3, as said below
- queries: bfloat16 [128, 4, 8192], P(('groups', 'section'), None, 'tensor'), parts along dimension 0, may hold values from -15 to 15
- new_kv: bfloat16 [128, 4, 2, 1024], P(('groups', 'section'), None, None, 'tensor'), parts along dimension 0, may hold values from -15 to 15
- block_table: int32 [128, 2], P(('groups', 'section')), parts along dimension 0, may hold values from 0 to 31, as said below
Outputs:
- kv_pool: bfloat16 [2, 256, 16, 1024], P(None, ('groups', 'section'), None, 'tensor'), parts along dimension 1
- decode_out: bfloat16 [128, 4, 8192], P(('groups', 'section'), None, 'tensor'), parts along dimension 0
The draws below stay inside these ranges and needn't reach their ends.
There are 2 independent parts, one for each index of `groups`. The reference program is written for one: setup_inputs(seed, part) draws one part's arguments, and reference() takes and returns one part's arrays. A program takes and returns all parts, laid end to end along the dimension named above; an argument that names none is the same for every part. Nothing has to cross between parts.
Inputs may be any that keep to these rules, and one draw needn't show every extreme that they name: `prompt_len`: some request has exactly 32. Every owner has exactly 16 requests. The 16 requests of one section index come in runs of 4 consecutive ones with one owner, and the runs of one index have different owners. `block_table`: the 16 rows of one owner's slots hold each of 0 .. 31 exactly once.
All inputs are finite; a program needn't handle non-finite values.
Results may differ from the reference program's by a relative error of at most 0.008.
Values may be sent and summed in bfloat16 or wider, within the bound.
A program may use at most 128 MiB of HBM per device.

```python
import jax
import jax.numpy as jnp
from jax import lax

D = 8192
KVH = 8
HD = 128
PMAX = 32
BLK = 16
STEPS = 4
REQ_DEV = 16
QPK = 8
REQUESTS = 64
MOST = 4
MAXB = 2
POOL = 32
N_SECTION = 4


def draw_queries(key, part):
    key = jax.random.fold_in(key, 7)
    fresh = jnp.clip(jax.random.normal(key, (REQUESTS, STEPS, KVH, QPK, HD), jnp.float32), -4.0, 4.0)
    return fresh.reshape(REQUESTS, STEPS, KVH * QPK * HD).astype(jnp.bfloat16)


def draw_new_kv(key, part):
    key = jax.random.fold_in(key, 9)
    fresh = jnp.clip(jax.random.normal(key, (REQUESTS, STEPS, 2, KVH, HD), jnp.float32), -4.0, 4.0)
    return fresh.reshape(REQUESTS, STEPS, 2, KVH * HD).astype(jnp.bfloat16)


def draw_prompt_len(key, part):
    key = jax.random.fold_in(key, 3)
    first_key, second_key = jax.random.split(key)
    drawn = jax.random.randint(first_key, (REQUESTS,), 1, PMAX + 1)
    longest = jax.random.randint(second_key, (), 0, REQUESTS)
    return jnp.where(jnp.arange(REQUESTS) == longest, PMAX, drawn).astype(jnp.int32)


def draw_owner(key, part):
    key = jax.random.fold_in(key, 5)
    first_key, second_key = jax.random.split(key)
    owners = REQUESTS // REQ_DEV
    shifts = jax.random.permutation(first_key, owners)
    relabel = jax.random.permutation(second_key, owners)
    request_ids = jnp.arange(REQUESTS)
    source = request_ids // REQ_DEV
    run_index = request_ids % REQ_DEV // MOST
    return relabel[(source + shifts[run_index]) % owners].astype(jnp.int32)


def permute_pool(owner_key):
    return jax.random.permutation(owner_key, POOL)


def draw_block_table(key, part):
    key = jax.random.fold_in(key, 4)
    owner_keys = jax.random.split(key, REQUESTS // REQ_DEV)
    tables = jax.vmap(permute_pool)(owner_keys)
    return tables.reshape(REQUESTS, MAXB).astype(jnp.int32)


def steps_of(key, shape, pieces, low, largest):
    level = 1.0
    for axis_at, shards_of in pieces:
        steps = jax.random.uniform(jax.random.fold_in(jax.random.fold_in(key, 6), axis_at), (shards_of,), jnp.float32, low / len(pieces), largest / len(pieces))
        level = level * jnp.repeat(jnp.exp(steps), shape[axis_at] // shards_of).reshape((-1,) + (1,) * (len(shape) - 1 - axis_at))
    return level


def bell_draw(own_key, extent, scale, limit, cuts=(), held_as=jnp.bfloat16):
    values = jax.random.normal(own_key, extent, jnp.float32) * scale
    if len(cuts) > 0:
        values = steps_of(own_key, extent, cuts, -0.22, 0.18) * values
    return jnp.clip(values, min=-limit, max=limit).astype(held_as)


def setup_inputs(seed: int = 0, part: int = 0) -> dict:
    arg_keys = jax.random.split(jax.random.key(seed), 9)
    part_splits = jax.random.split(jax.random.fold_in(arg_keys[8], part), 9)
    return {
        "hidden": bell_draw(part_splits[0], (REQUESTS, PMAX, D), 1.0, 6.0, ((0, 4), (2, 4))),
        "kv_weight": bell_draw(arg_keys[1], (D, 2, KVH * HD), D ** -0.5, 0.0625, ((2, 4),)),
        "kv_bias": bell_draw(arg_keys[2], (2, KVH * HD), 0.5, 3.0, ((1, 4),)),
        "prompt_len": draw_prompt_len(jax.random.fold_in(jax.random.fold_in(arg_keys[8], part), 71), part),
        "owner": draw_owner(jax.random.fold_in(jax.random.fold_in(arg_keys[8], part), 71), part),
        "queries": draw_queries(jax.random.fold_in(jax.random.fold_in(arg_keys[8], part), 71), part),
        "new_kv": draw_new_kv(jax.random.fold_in(jax.random.fold_in(arg_keys[8], part), 71), part),
        "block_table": draw_block_table(jax.random.fold_in(jax.random.fold_in(arg_keys[8], part), 71), part),
    }


rope_base = 1000000.0


def rotary(key_rows, offset):
    half_dim = key_rows.shape[-1] // 2
    row_count = key_rows.shape[-3]
    positions = (jnp.arange(row_count) + offset).astype(jnp.float32)
    inverse = rope_base ** (-(jnp.arange(half_dim).astype(jnp.float32) * 2.0 / key_rows.shape[-1]))
    angles = positions[:, None] * inverse[None, :]
    cosine = jnp.concatenate([jnp.cos(angles), jnp.cos(angles)], axis=-1)[:, None, :]
    sine_part = jnp.concatenate([jnp.sin(angles), jnp.sin(angles)], axis=-1)[:, None, :]
    turned = jnp.concatenate([-key_rows[..., half_dim:], key_rows[..., :half_dim]], axis=-1)
    return key_rows * cosine + turned * sine_part


def finish(partial_value, kv_bias, offset, lengths, groups):
    span_len = partial_value.shape[1]
    biased = partial_value + kv_bias.astype(jnp.float32).reshape(2, groups, HD)
    rotated = rotary(biased[:, :, 0], offset)
    merged = jnp.stack([rotated, biased[:, :, 1]], axis=2)
    positions = jnp.arange(span_len) + offset
    live_rows = positions[None, :] < lengths[:, None]
    return jnp.where(live_rows[:, :, None, None, None], merged, 0.0).astype(jnp.bfloat16)


def attend(query_rows, slot_kv, new_kv, slot_len, groups):
    slot_count = query_rows.shape[0]
    queries = query_rows.astype(jnp.float32).reshape(slot_count, STEPS, groups, QPK, HD)
    cached = slot_kv.astype(jnp.float32).reshape(slot_count, -1, 2, groups, HD)
    recent = new_kv.astype(jnp.float32).reshape(slot_count, STEPS, 2, groups, HD)
    score_scale = HD ** -0.5
    old_scores = jnp.einsum("rtgqd,rpgd->rtgqp", queries, cached[:, :, 0]) * score_scale
    new_scores = jnp.einsum("rtgqd,rsgd->rtgqs", queries, recent[:, :, 0]) * score_scale
    prompt_slots = cached.shape[1]
    prompt_pos = jnp.arange(prompt_slots)
    old_live = (prompt_pos[None, :] < slot_len[:, None])[:, None, None, None, :]
    step_pos = jnp.arange(STEPS)
    new_live = (step_pos[None, :] <= step_pos[:, None])[None, :, None, None, :]
    scores = jnp.concatenate([jnp.where(old_live, old_scores, -jnp.inf), jnp.where(new_live, new_scores, -jnp.inf)], axis=-1)
    attn_probs = jax.nn.softmax(scores, axis=-1).astype(jnp.bfloat16).astype(jnp.float32)
    attended = jnp.einsum("rtgqp,rpgd->rtgqd", attn_probs[..., :prompt_slots], cached[:, :, 1])
    attended = attended + jnp.einsum("rtgqs,rsgd->rtgqd", attn_probs[..., prompt_slots:], recent[:, :, 1])
    return attended.astype(jnp.bfloat16).reshape(slot_count, STEPS, groups * QPK * HD)


def place_blocks(block_rows, table_row):
    return jnp.zeros_like(block_rows).at[table_row].set(block_rows)


def reference(hidden, kv_weight, kv_bias, prompt_len, owner, queries, new_kv, block_table):
    weight_mat = kv_weight.reshape(D, 2 * KVH * HD)

    def project_block(inputs):
        rows_in, lens_in = inputs
        partial_value = jnp.dot(rows_in.reshape(REQ_DEV * PMAX, D), weight_mat, preferred_element_type=jnp.float32)
        return finish(partial_value.reshape(REQ_DEV, PMAX, 2, KVH, HD), kv_bias, 0, lens_in, KVH)

    prompt_kv = lax.map(project_block, (hidden.reshape(N_SECTION, REQ_DEV, PMAX, D), prompt_len.reshape(N_SECTION, REQ_DEV)))
    prompt_kv = prompt_kv.reshape(REQUESTS, PMAX, 2, KVH * HD)
    slot_order = jnp.argsort(owner, stable=True).astype(jnp.int32)
    slot_kv = prompt_kv[slot_order]
    slot_len = prompt_len[slot_order]
    blocks = slot_kv.reshape(N_SECTION, POOL, BLK, 2, KVH * HD)
    tables = block_table.reshape(N_SECTION, POOL)
    pooled = jax.vmap(place_blocks)(blocks, tables)
    kv_pool = jnp.transpose(pooled, (3, 0, 1, 2, 4)).reshape(2, N_SECTION * POOL, BLK, KVH * HD)
    decode_out = attend(queries, slot_kv, new_kv, slot_len, KVH)
    return (kv_pool, decode_out)
```

```python
import jax
import jax.numpy as jnp
from jax import lax
from jax.experimental import pallas as pl
from jax.experimental.pallas import tpu as pltpu
from jax.sharding import PartitionSpec as P

HD = 128
BLK = 16
STEPS = 4
QPK = 8


rope_base = 1000000.0


def rotary(key_rows, offset):
    half_dim = key_rows.shape[-1] // 2
    row_count = key_rows.shape[-3]
    positions = (jnp.arange(row_count) + offset).astype(jnp.float32)
    inverse = rope_base ** (-(jnp.arange(half_dim).astype(jnp.float32) * 2.0 / key_rows.shape[-1]))
    angles = positions[:, None] * inverse[None, :]
    cosine = jnp.concatenate([jnp.cos(angles), jnp.cos(angles)], axis=-1)[:, None, :]
    sine_part = jnp.concatenate([jnp.sin(angles), jnp.sin(angles)], axis=-1)[:, None, :]
    turned = jnp.concatenate([-key_rows[..., half_dim:], key_rows[..., :half_dim]], axis=-1)
    return key_rows * cosine + turned * sine_part


def finish(partial_value, kv_bias, offset, lengths, groups):
    span_len = partial_value.shape[1]
    biased = partial_value + kv_bias.astype(jnp.float32).reshape(2, groups, HD)
    rotated = rotary(biased[:, :, 0], offset)
    merged = jnp.stack([rotated, biased[:, :, 1]], axis=2)
    positions = jnp.arange(span_len) + offset
    live_rows = positions[None, :] < lengths[:, None]
    return jnp.where(live_rows[:, :, None, None, None], merged, 0.0).astype(jnp.bfloat16)


def folder(weight_mat):

    def add_slab(running, slab, first_col):
        col_count = slab.shape[-1]
        return jnp.dot(slab.reshape(-1, col_count), weight_mat, preferred_element_type=jnp.float32)

    return add_slab


def attend(query_rows, slot_kv, new_kv, slot_len, groups):
    slot_count = query_rows.shape[0]
    queries = query_rows.reshape(slot_count, STEPS, groups, QPK, HD)
    cached = slot_kv.reshape(slot_count, -1, 2, groups, HD)
    recent = new_kv.reshape(slot_count, STEPS, 2, groups, HD)
    score_scale = HD ** (-0.5)
    old_scores = (
        jnp.einsum(
            "rtgqd,rpgd->rtgqp", queries, cached[:, :, 0], preferred_element_type=jnp.float32
        )
        * score_scale
    )
    new_scores = (
        jnp.einsum(
            "rtgqd,rsgd->rtgqs", queries, recent[:, :, 0], preferred_element_type=jnp.float32
        )
        * score_scale
    )
    prompt_slots = cached.shape[1]
    prompt_pos = jnp.arange(prompt_slots)
    old_live = (prompt_pos[None, :] < slot_len[:, None])[:, None, None, None, :]
    step_pos = jnp.arange(STEPS)
    new_live = (step_pos[None, :] <= step_pos[:, None])[None, :, None, None, :]
    scores = jnp.concatenate(
        [jnp.where(old_live, old_scores, -jnp.inf), jnp.where(new_live, new_scores, -jnp.inf)],
        axis=-1,
    )
    attn_probs = jax.nn.softmax(scores, axis=-1).astype(jnp.bfloat16)
    attended = jnp.einsum(
        "rtgqp,rpgd->rtgqd",
        attn_probs[..., :prompt_slots],
        cached[:, :, 1],
        preferred_element_type=jnp.float32,
    )
    attended = attended + jnp.einsum(
        "rtgqs,rsgd->rtgqd",
        attn_probs[..., prompt_slots:],
        recent[:, :, 1],
        preferred_element_type=jnp.float32,
    )
    return attended.astype(jnp.bfloat16).reshape(slot_count, STEPS, groups * QPK * HD)


def per_device_general(hidden, kv_weight, kv_bias, prompt_len, owner, queries, new_kv, block_table):
    n_section = lax.axis_size("section")
    own_index = lax.axis_index("section")
    req_count = hidden.shape[0]
    prompt_max = hidden.shape[1]
    kv_width = kv_weight.shape[2]
    groups = kv_width // HD
    run_most = max(2, req_count // n_section)
    owner_grid = owner.reshape(n_section, req_count)
    local_owner = lax.dynamic_index_in_dim(owner_grid, own_index, 0, keepdims=False)
    local_len = lax.dynamic_slice_in_dim(prompt_len, own_index * req_count, req_count)
    local_ids = jnp.arange(req_count)
    earlier = (local_owner[:, None] == local_owner[None, :]) & (
        local_ids[None, :] < local_ids[:, None]
    )
    send_pos = local_owner * run_most + jnp.sum(earlier.astype(jnp.int32), axis=1)
    run_rank = jnp.cumsum((owner_grid == own_index).astype(jnp.int32), axis=1) - 1
    slot_order = jnp.argsort(owner, stable=True)
    own_slots = lax.dynamic_slice_in_dim(slot_order, own_index * req_count, req_count)
    recv_pos = own_slots // req_count * run_most + run_rank.reshape(-1)[own_slots]
    slot_len = prompt_len[own_slots]
    weight_mat = kv_weight.reshape(kv_weight.shape[0], 2 * kv_width)
    add_slab = folder(weight_mat)
    blank_acc = jnp.zeros((req_count * prompt_max, 2 * kv_width), jnp.float32)
    partial_value = add_slab(
        blank_acc, lax.all_gather(hidden, "tensor", axis=2, tiled=True), jnp.int32(0)
    )
    span_len = partial_value.shape[0] // req_count
    shaped = partial_value.reshape(req_count, span_len, 2, groups, HD)
    kv_rows = finish(shaped, kv_bias, 0, local_len, groups).reshape(
        req_count, span_len, 2, kv_width
    )
    blank_buf = jnp.zeros((n_section * run_most,) + kv_rows.shape[1:], kv_rows.dtype)
    arrived = lax.all_to_all(
        blank_buf.at[send_pos].set(kv_rows), "section", split_axis=0, concat_axis=0, tiled=True
    )
    slot_kv = jnp.take(arrived, recv_pos, axis=0)
    decode_out = attend(queries, slot_kv, new_kv, slot_len, groups)
    block_count = prompt_max // BLK
    blocks = slot_kv.reshape(req_count * block_count, BLK, 2, kv_width)
    pool_rows = jnp.zeros_like(blocks).at[block_table.reshape(-1)].set(blocks)
    return (jnp.transpose(pool_rows, (2, 0, 1, 3)), decode_out)

MESH = pl.DeviceIdType.MESH
RUNS = 4


def partner_of(me, step):
    if step == 0:
        return 3 - me
    if step == 1:
        return lax.rem(me + 2, 4)
    if step == 2:
        return me + 1 - 2 * lax.rem(me, 2)
    return me


def routed_kernel(
    h0, h1, h2, h3, x0, w_hbm, bias_ref, cos_ref, sin_ref, live_ref, lencol_ref, inv_ref, q_ref, new_ref,
    pool_ref, out_ref,
    gathered, weight, kvbuf, sendbuf,
    w_sem, own_sem, x0_sem, sib_send, sib_recv, x_send, x_recv, fwd_send, fwd_recv, z_send, z_recv,
):
    hidden = (h0, h1, h2, h3)
    sec = lax.axis_index("section")
    me = lax.axis_index("tensor")
    sib = me + 1 - 2 * lax.rem(me, 2)
    across = lax.rem(me + 2, 4)
    across_sib = lax.rem(sib + 2, 4)
    order = (me, sib, across, across_sib)
    rows = gathered.shape[2]

    barrier = pltpu.get_barrier_semaphore()
    pl.semaphore_signal(barrier, inc=1, device_id={"tensor": sib}, device_id_type=MESH)
    pl.semaphore_signal(barrier, inc=1, device_id={"tensor": across}, device_id_type=MESH)
    for step in range(3):
        pl.semaphore_signal(
            barrier, inc=1, device_id={"section": partner_of(sec, step)}, device_id_type=MESH
        )
    w_copies = [
        pltpu.make_async_copy(w_hbm.at[:, t], weight.at[:, t], w_sem.at[i])
        for i, t in enumerate(order)
    ]
    own_copies = [
        pltpu.make_async_copy(hidden[j], gathered.at[j, me], own_sem.at[j]) for j in range(RUNS)
    ]
    x0_copy = pltpu.make_async_copy(x0, gathered.at[0, across], x0_sem)
    pl.semaphore_wait(barrier, 5)

    def remote(src, dst, send, recv, where):
        return pltpu.make_async_remote_copy(
            src_ref=src, dst_ref=dst, send_sem=send, recv_sem=recv, device_id=where, device_id_type=MESH
        )

    x_copies = [None] + [
        remote(hidden[j], gathered.at[j, me], x_send.at[j], x_recv.at[j], {"tensor": across})
        for j in range(1, RUNS)
    ]
    sib_copies = [
        remote(hidden[j], gathered.at[j, me], sib_send.at[j], sib_recv.at[j], {"tensor": sib})
        for j in range(RUNS)
    ]
    fwd_copies = [
        remote(
            x0 if j == 0 else gathered.at[j, across],
            gathered.at[j, across],
            fwd_send.at[j],
            fwd_recv.at[j],
            {"tensor": sib},
        )
        for j in range(RUNS)
    ]
    x_copies[1].start()
    sib_copies[0].start()
    fwd_copies[0].start()
    x_copies[2].start()
    w_copies[0].start()
    own_copies[0].start()
    w_copies[1].start()
    x0_copy.start()
    w_copies[2].start()
    w_copies[3].start()
    for j in range(1, RUNS):
        own_copies[j].start()
        sib_copies[j].start()

    def half(j, t):
        a = gathered[j, t]
        return (
            jnp.dot(a, weight[0, t], preferred_element_type=jnp.float32),
            jnp.dot(a, weight[1, t], preferred_element_type=jnp.float32),
        )

    row = lax.broadcasted_iota(jnp.int32, (128, 128), 0)
    col = lax.broadcasted_iota(jnp.int32, (128, 128), 1)
    same_slot = (row // 32) == (col // 32)
    row16 = lax.broadcasted_iota(jnp.int32, (128, 16), 0)
    col16 = lax.broadcasted_iota(jnp.int32, (128, 16), 1)
    new_live = ((row16 // 32) == (col16 // 4)) & ((col16 % 4) <= ((row16 % 32) // 8))
    contract = (((1,), (1,)), ((), ()))

    def attend_run(s):
        old_live = same_slot & ((col % 32) < lencol_ref[s])
        for g in range(2):
            q = q_ref[g, s]
            kv = kvbuf[pl.ds(8 * s, 8)].reshape(128, 512)
            k = kv[:, g * 128 : (g + 1) * 128]
            v = kv[:, 256 + g * 128 : 256 + (g + 1) * 128]
            old = lax.dot_general(q, k, contract, preferred_element_type=jnp.float32) * HD ** (-0.5)
            new = (
                lax.dot_general(q, new_ref[0, g, s], contract, preferred_element_type=jnp.float32)
                * HD ** (-0.5)
            )
            old = jnp.where(old_live, old, -jnp.inf)
            new = jnp.where(new_live, new, -jnp.inf)
            top = jnp.maximum(
                jnp.max(old, axis=1, keepdims=True), jnp.max(new, axis=1, keepdims=True)
            )
            old = jnp.exp(old - top)
            new = jnp.exp(new - top)
            total = jnp.sum(old, axis=1, keepdims=True) + jnp.sum(new, axis=1, keepdims=True)
            old = (old / total).astype(jnp.bfloat16)
            new = (new / total).astype(jnp.bfloat16)
            res = jnp.dot(old, v, preferred_element_type=jnp.float32) + jnp.dot(
                new, new_ref[1, g, s], preferred_element_type=jnp.float32
            )
            out_ref[g, s] = res.astype(jnp.bfloat16)

    z_copies = []
    for j in range(RUNS):
        if j > 0:
            x_copies[j].wait_recv()
            fwd_copies[j].start()
            if j + 2 < RUNS:
                x_copies[j + 2].start()
        own_copies[j].wait()
        if j == 0:
            w_copies[0].wait()
        k_acc, v_acc = half(j, me)
        sib_copies[j].wait_recv()
        if j == 0:
            w_copies[1].wait()
        k_one, v_one = half(j, sib)
        k_acc, v_acc = k_acc + k_one, v_acc + v_one
        if j == 0:
            x0_copy.wait()
            w_copies[2].wait()
        k_one, v_one = half(j, across)
        k_acc, v_acc = k_acc + k_one, v_acc + v_one
        fwd_copies[j].wait_recv()
        if j == 0:
            w_copies[3].wait()
        k_one, v_one = half(j, across_sib)
        k_acc, v_acc = k_acc + k_one, v_acc + v_one
        k_acc = k_acc + bias_ref[0:1, :]
        v_acc = v_acc + bias_ref[1:2, :]
        live = live_ref[j] > 0
        parts = []
        for g in range(2):
            k = k_acc[:, g * 128 : (g + 1) * 128]
            k = k * cos_ref[...] + pltpu.roll(k, 64, 1) * sin_ref[...]
            parts.append(jnp.where(live, k, 0.0).astype(jnp.bfloat16))
        for g in range(2):
            parts.append(jnp.where(live, v_acc[:, g * 128 : (g + 1) * 128], 0.0).astype(jnp.bfloat16))
        done = jnp.concatenate(parts, axis=1).reshape(8, 16, 512)
        if j < RUNS - 1:
            sendbuf[j] = done
            copy = remote(
                sendbuf.at[j],
                kvbuf.at[pl.ds(8 * sec, 8)],
                z_send.at[j],
                z_recv.at[j],
                {"section": partner_of(sec, j)},
            )
            copy.start()
            z_copies.append(copy)
        else:
            kvbuf[pl.ds(8 * sec, 8)] = done
        if j > 0:
            z_copies[j - 1].wait_recv()
            attend_run(partner_of(sec, j - 1))
    attend_run(sec)
    for block in range(pool_ref.shape[1]):
        rows_in = kvbuf[inv_ref[block]]
        pool_ref[0, block] = rows_in[:, :256]
        pool_ref[1, block] = rows_in[:, 256:]
    for j in range(RUNS):
        sib_copies[j].wait_send()
        fwd_copies[j].wait_send()
        if j > 0:
            x_copies[j].wait_send()
        if j < RUNS - 1:
            z_copies[j].wait_send()


def per_device_routed(hidden, kv_weight, kv_bias, prompt_len, owner, queries, new_kv, block_table):
    sec = lax.axis_index("section")
    req_count, prompt_max, feats = hidden.shape
    run = req_count // RUNS
    rows = run * prompt_max
    run_owner = owner.reshape(-1, RUNS, run)[:, :, 0]
    run_ids = jnp.arange(RUNS)
    own_runs = lax.dynamic_index_in_dim(run_owner, sec, 0, keepdims=False)
    lengths = prompt_len.reshape(-1, RUNS, run)
    own_len = lax.dynamic_index_in_dim(lengths, sec, 0, keepdims=False)
    picks = [jnp.sum(jnp.where(own_runs == partner_of(sec, j), run_ids, 0)) for j in range(RUNS)]
    by_run = hidden.reshape(RUNS, rows, feats)
    parts = [lax.dynamic_index_in_dim(by_run, pick, 0, keepdims=False) for pick in picks]
    across = lax.ppermute(parts[0], "tensor", [(t, (t + 2) % 4) for t in range(4)])
    weight = kv_weight.reshape(4, feats, 2, 256).transpose(2, 0, 1, 3)
    picked_len = jnp.stack([lax.dynamic_index_in_dim(own_len, p, 0, keepdims=False) for p in picks])
    positions = jnp.arange(prompt_max)
    live = (positions[None, None, :] < picked_len[:, :, None]).astype(jnp.float32)
    live = jnp.broadcast_to(live.reshape(RUNS, rows, 1), (RUNS, rows, HD))
    mine = (run_owner == sec)[:, :, None]
    slot_len = jnp.sum(jnp.where(mine, lengths, 0), axis=1)
    lencol = jnp.repeat(slot_len, prompt_max, axis=1).reshape(-1, 1, rows)
    table = block_table.reshape(-1)
    count = table.shape[0]
    inverse = jnp.sum(
        jnp.where(table[None, :] == jnp.arange(count)[:, None], jnp.arange(count)[None, :], 0), axis=1
    ).astype(jnp.int32)
    freq = rope_base ** (-(jnp.arange(HD // 2).astype(jnp.float32) * 2.0 / HD))
    angles = positions.astype(jnp.float32)[:, None] * freq[None, :]
    cosine = jnp.concatenate([jnp.cos(angles), jnp.cos(angles)], axis=-1)
    sine = jnp.concatenate([-jnp.sin(angles), jnp.sin(angles)], axis=-1)
    cosine = jnp.tile(cosine, (run, 1))
    sine = jnp.tile(sine, (run, 1))
    bias = kv_bias.astype(jnp.float32)
    q = queries.reshape(4, run, STEPS, 2, QPK, HD).transpose(3, 0, 1, 2, 4, 5).reshape(2, 4, rows, HD)
    new = new_kv.reshape(4, run, STEPS, 2, 2, HD).transpose(3, 4, 0, 1, 2, 5)
    new = new.reshape(2, 2, 4, run * STEPS, HD)
    vmem = pl.BlockSpec(memory_space=pltpu.VMEM)
    anym = pl.BlockSpec(memory_space=pl.ANY)
    dma = pltpu.SemaphoreType.DMA
    pool, out = pl.pallas_call(
        routed_kernel,
        out_shape=(
            jax.ShapeDtypeStruct((2, count, BLK, 256), jnp.bfloat16),
            jax.ShapeDtypeStruct((2, 4, rows, HD), jnp.bfloat16),
        ),
        in_specs=[anym] * 6 + [vmem] * 5 + [pl.BlockSpec(memory_space=pltpu.SMEM)] + [vmem] * 2,
        out_specs=(vmem, vmem),
        scratch_shapes=[
            pltpu.VMEM((RUNS, 4, rows, feats), jnp.bfloat16),
            pltpu.VMEM((2, 4, feats, 256), jnp.bfloat16),
            pltpu.VMEM((count, BLK, 512), jnp.bfloat16),
            pltpu.VMEM((RUNS - 1, 8, BLK, 512), jnp.bfloat16),
            dma((4,)),
            dma((RUNS,)),
            dma,
            dma((RUNS,)),
            dma((RUNS,)),
            dma((RUNS,)),
            dma((RUNS,)),
            dma((RUNS,)),
            dma((RUNS,)),
            dma((RUNS,)),
            dma((RUNS,)),
        ],
        compiler_params=pltpu.CompilerParams(
            collective_id=0, has_side_effects=True, vmem_limit_bytes=40 * 1024 * 1024
        ),
        cost_estimate=pl.CostEstimate(
            flops=2 * RUNS * rows * 4 * feats * 512, bytes_accessed=16 * 1024 * 1024, transcendentals=0
        ),
    )(*parts, across, weight, bias, cosine, sine, live, lencol, inverse, q, new)
    out = out.reshape(2, 4, run, STEPS, QPK, HD).transpose(1, 2, 3, 0, 4, 5)
    return (pool, out.reshape(req_count, STEPS, 2 * QPK * HD))


def solution(mesh):
    routed = mesh.shape["section"] == RUNS and mesh.shape["tensor"] == 4
    per_device = per_device_routed if routed else per_device_general
    return jax.shard_map(
        per_device,
        mesh=mesh,
        in_specs=(
            P(("groups", "section"), None, "tensor"),
            P(None, None, "tensor"),
            P(None, "tensor"),
            P("groups"),
            P("groups"),
            P(("groups", "section"), None, "tensor"),
            P(("groups", "section"), None, None, "tensor"),
            P(("groups", "section"), None),
        ),
        out_specs=(
            P(None, ("groups", "section"), None, "tensor"),
            P(("groups", "section"), None, "tensor"),
        ),
        check_vma=False,
    )
```

```python
import functools

import jax
import jax.numpy as jnp
from jax import lax
from jax.experimental import pallas as pl
from jax.experimental.pallas import tpu as pltpu
from jax.sharding import PartitionSpec as P

HD = 128
BLK = 16
STEPS = 4
QPK = 8


rope_base = 1000000.0


def rotary(key_rows, offset):
    half_dim = key_rows.shape[-1] // 2
    row_count = key_rows.shape[-3]
    positions = (jnp.arange(row_count) + offset).astype(jnp.float32)
    inverse = rope_base ** (-(jnp.arange(half_dim).astype(jnp.float32) * 2.0 / key_rows.shape[-1]))
    angles = positions[:, None] * inverse[None, :]
    cosine = jnp.concatenate([jnp.cos(angles), jnp.cos(angles)], axis=-1)[:, None, :]
    sine_part = jnp.concatenate([jnp.sin(angles), jnp.sin(angles)], axis=-1)[:, None, :]
    turned = jnp.concatenate([-key_rows[..., half_dim:], key_rows[..., :half_dim]], axis=-1)
    return key_rows * cosine + turned * sine_part


def finish(partial_value, kv_bias, offset, lengths, groups):
    span_len = partial_value.shape[1]
    biased = partial_value + kv_bias.astype(jnp.float32).reshape(2, groups, HD)
    rotated = rotary(biased[:, :, 0], offset)
    merged = jnp.stack([rotated, biased[:, :, 1]], axis=2)
    positions = jnp.arange(span_len) + offset
    live_rows = positions[None, :] < lengths[:, None]
    return jnp.where(live_rows[:, :, None, None, None], merged, 0.0).astype(jnp.bfloat16)


def folder(weight_mat):

    def add_slab(running, slab, first_col):
        col_count = slab.shape[-1]
        return jnp.dot(slab.reshape(-1, col_count), weight_mat, preferred_element_type=jnp.float32)

    return add_slab


def attend(query_rows, slot_kv, new_kv, slot_len, groups):
    slot_count = query_rows.shape[0]
    queries = query_rows.reshape(slot_count, STEPS, groups, QPK, HD)
    cached = slot_kv.reshape(slot_count, -1, 2, groups, HD)
    recent = new_kv.reshape(slot_count, STEPS, 2, groups, HD)
    score_scale = HD ** (-0.5)
    old_scores = (
        jnp.einsum(
            "rtgqd,rpgd->rtgqp", queries, cached[:, :, 0], preferred_element_type=jnp.float32
        )
        * score_scale
    )
    new_scores = (
        jnp.einsum(
            "rtgqd,rsgd->rtgqs", queries, recent[:, :, 0], preferred_element_type=jnp.float32
        )
        * score_scale
    )
    prompt_slots = cached.shape[1]
    prompt_pos = jnp.arange(prompt_slots)
    old_live = (prompt_pos[None, :] < slot_len[:, None])[:, None, None, None, :]
    step_pos = jnp.arange(STEPS)
    new_live = (step_pos[None, :] <= step_pos[:, None])[None, :, None, None, :]
    scores = jnp.concatenate(
        [jnp.where(old_live, old_scores, -jnp.inf), jnp.where(new_live, new_scores, -jnp.inf)],
        axis=-1,
    )
    attn_probs = jax.nn.softmax(scores, axis=-1).astype(jnp.bfloat16)
    attended = jnp.einsum(
        "rtgqp,rpgd->rtgqd",
        attn_probs[..., :prompt_slots],
        cached[:, :, 1],
        preferred_element_type=jnp.float32,
    )
    attended = attended + jnp.einsum(
        "rtgqs,rsgd->rtgqd",
        attn_probs[..., prompt_slots:],
        recent[:, :, 1],
        preferred_element_type=jnp.float32,
    )
    return attended.astype(jnp.bfloat16).reshape(slot_count, STEPS, groups * QPK * HD)


def per_device_general(hidden, kv_weight, kv_bias, prompt_len, owner, queries, new_kv, block_table):
    n_section = lax.axis_size("section")
    own_index = lax.axis_index("section")
    req_count = hidden.shape[0]
    prompt_max = hidden.shape[1]
    kv_width = kv_weight.shape[2]
    groups = kv_width // HD
    run_most = max(2, req_count // n_section)
    owner_grid = owner.reshape(n_section, req_count)
    local_owner = lax.dynamic_index_in_dim(owner_grid, own_index, 0, keepdims=False)
    local_len = lax.dynamic_slice_in_dim(prompt_len, own_index * req_count, req_count)
    local_ids = jnp.arange(req_count)
    earlier = (local_owner[:, None] == local_owner[None, :]) & (
        local_ids[None, :] < local_ids[:, None]
    )
    send_pos = local_owner * run_most + jnp.sum(earlier.astype(jnp.int32), axis=1)
    run_rank = jnp.cumsum((owner_grid == own_index).astype(jnp.int32), axis=1) - 1
    slot_order = jnp.argsort(owner, stable=True)
    own_slots = lax.dynamic_slice_in_dim(slot_order, own_index * req_count, req_count)
    recv_pos = own_slots // req_count * run_most + run_rank.reshape(-1)[own_slots]
    slot_len = prompt_len[own_slots]
    weight_mat = kv_weight.reshape(kv_weight.shape[0], 2 * kv_width)
    add_slab = folder(weight_mat)
    blank_acc = jnp.zeros((req_count * prompt_max, 2 * kv_width), jnp.float32)
    partial_value = add_slab(
        blank_acc, lax.all_gather(hidden, "tensor", axis=2, tiled=True), jnp.int32(0)
    )
    span_len = partial_value.shape[0] // req_count
    shaped = partial_value.reshape(req_count, span_len, 2, groups, HD)
    kv_rows = finish(shaped, kv_bias, 0, local_len, groups).reshape(
        req_count, span_len, 2, kv_width
    )
    blank_buf = jnp.zeros((n_section * run_most,) + kv_rows.shape[1:], kv_rows.dtype)
    arrived = lax.all_to_all(
        blank_buf.at[send_pos].set(kv_rows), "section", split_axis=0, concat_axis=0, tiled=True
    )
    slot_kv = jnp.take(arrived, recv_pos, axis=0)
    decode_out = attend(queries, slot_kv, new_kv, slot_len, groups)
    block_count = prompt_max // BLK
    blocks = slot_kv.reshape(req_count * block_count, BLK, 2, kv_width)
    pool_rows = jnp.zeros_like(blocks).at[block_table.reshape(-1)].set(blocks)
    return (jnp.transpose(pool_rows, (2, 0, 1, 3)), decode_out)

MESH = pl.DeviceIdType.MESH
RUNS = 4


def partner_of(me, step):
    if step == 0:
        return 3 - me
    if step == 1:
        return lax.rem(me + 2, 4)
    if step == 2:
        return me + 1 - 2 * lax.rem(me, 2)
    return me


def routed_kernel(
    head, h_ref, x0_ref, w_hbm, bias_ref, cos_ref, sin_ref, owner_ref, len_ref, inv_ref, q_ref, new_ref,
    pool_ref, out_ref,
    gathered, weight, kvbuf, sendbuf,
    w_sem, sib_send, sib_recv, x_send, x_recv, head_send, head_recv, fwd_send, fwd_recv, z_send, z_recv,
):
    sec = lax.axis_index("section")
    me = lax.axis_index("tensor")
    sib = me + 1 - 2 * lax.rem(me, 2)
    across = lax.rem(me + 2, 4)
    across_sib = lax.rem(sib + 2, 4)
    order = (me, sib, across, across_sib)
    rest = gathered.shape[3] - head

    barrier = pltpu.get_barrier_semaphore()
    pl.semaphore_signal(barrier, inc=1, device_id={"tensor": sib}, device_id_type=MESH)
    pl.semaphore_signal(barrier, inc=1, device_id={"tensor": across}, device_id_type=MESH)
    for step in range(3):
        pl.semaphore_signal(
            barrier, inc=1, device_id={"section": partner_of(sec, step)}, device_id_type=MESH
        )
    w_copies = [
        pltpu.make_async_copy(w_hbm.at[:, t], weight.at[:, t], w_sem.at[i])
        for i, t in enumerate(order)
    ]

    def run_of(source, target):
        found = jnp.int32(0)
        for r in range(1, RUNS):
            found = jnp.where(owner_ref[source * 16 + r * 4] == target, r, found)
        return found

    runs = [run_of(sec, partner_of(sec, j)) for j in range(RUNS)]

    def remote(src, dst, send, recv, where):
        return pltpu.make_async_remote_copy(
            src_ref=src, dst_ref=dst, send_sem=send, recv_sem=recv, device_id=where, device_id_type=MESH
        )

    def same(slot, send, recv, where):
        return remote(slot, slot, send, recv, where)

    tail = pl.ds(head, rest)
    x_copies = [
        same(gathered.at[j, me, :, tail], x_send.at[j], x_recv.at[j], {"tensor": across})
        for j in range(RUNS)
    ]
    sib_copies = [
        same(gathered.at[j, me], sib_send.at[j], sib_recv.at[j], {"tensor": sib}) for j in range(RUNS)
    ]
    head_copies = [
        same(
            gathered.at[j, across, :, pl.ds(0, head)], head_send.at[j], head_recv.at[j], {"tensor": sib}
        )
        for j in range(RUNS)
    ]
    fwd_copies = [
        same(gathered.at[j, across, :, tail], fwd_send.at[j], fwd_recv.at[j], {"tensor": sib})
        for j in range(RUNS)
    ]
    gathered[0, me] = h_ref[runs[0]]
    pl.semaphore_wait(barrier, 5)
    x_copies[0].start()
    gathered[1, me] = h_ref[runs[1]]
    x_copies[1].start()
    w_copies[0].start()
    w_copies[1].start()
    sib_copies[0].start()
    gathered[0, across, :, 0:head] = x0_ref[runs[0]]
    head_copies[0].start()
    w_copies[2].start()
    w_copies[3].start()
    for j in range(1, RUNS):
        if j > 1:
            gathered[j, me] = h_ref[runs[j]]
        sib_copies[j].start()
        gathered[j, across, :, 0:head] = x0_ref[runs[j]]
        head_copies[j].start()

    def half(j, t):
        a = gathered[j, t]
        return (
            jnp.dot(a, weight[0, t], preferred_element_type=jnp.float32),
            jnp.dot(a, weight[1, t], preferred_element_type=jnp.float32),
        )

    row = lax.broadcasted_iota(jnp.int32, (128, 128), 0)
    col = lax.broadcasted_iota(jnp.int32, (128, 128), 1)
    same_slot = (row // 32) == (col // 32)
    row16 = lax.broadcasted_iota(jnp.int32, (128, 16), 0)
    col16 = lax.broadcasted_iota(jnp.int32, (128, 16), 1)
    new_live = ((row16 // 32) == (col16 // 4)) & ((col16 % 4) <= ((row16 % 32) // 8))
    contract = (((1,), (1,)), ((), ()))

    def within(index, source, run):
        first = source * 16 + run * 4
        limit = jnp.full(index.shape, len_ref[first], jnp.int32)
        for i in range(1, 4):
            limit = jnp.where(index // 32 == i, len_ref[first + i], limit)
        return (index % 32) < limit

    def attend_run(s):
        old_live = same_slot & within(col, s, run_of(s, sec))
        for g in range(2):
            q = q_ref[g, s]
            kv = kvbuf[pl.ds(8 * s, 8)].reshape(128, 512)
            k = kv[:, g * 128 : (g + 1) * 128]
            v = kv[:, 256 + g * 128 : 256 + (g + 1) * 128]
            old = lax.dot_general(q, k, contract, preferred_element_type=jnp.float32) * HD ** (-0.5)
            new = (
                lax.dot_general(q, new_ref[0, g, s], contract, preferred_element_type=jnp.float32)
                * HD ** (-0.5)
            )
            old = jnp.where(old_live, old, -jnp.inf)
            new = jnp.where(new_live, new, -jnp.inf)
            top = jnp.maximum(
                jnp.max(old, axis=1, keepdims=True), jnp.max(new, axis=1, keepdims=True)
            )
            old = jnp.exp(old - top)
            new = jnp.exp(new - top)
            total = jnp.sum(old, axis=1, keepdims=True) + jnp.sum(new, axis=1, keepdims=True)
            old = (old / total).astype(jnp.bfloat16)
            new = (new / total).astype(jnp.bfloat16)
            res = jnp.dot(old, v, preferred_element_type=jnp.float32) + jnp.dot(
                new, new_ref[1, g, s], preferred_element_type=jnp.float32
            )
            out_ref[g, s] = res.astype(jnp.bfloat16)

    bias = bias_ref[...].astype(jnp.float32)
    z_copies = []
    for j in range(RUNS):
        if j == 0:
            w_copies[0].wait()
        k_acc, v_acc = half(j, me)
        sib_copies[j].wait_recv()
        if j == 0:
            w_copies[1].wait()
        k_one, v_one = half(j, sib)
        k_acc, v_acc = k_acc + k_one, v_acc + v_one
        if j > 0:
            z_copies[j - 1].wait_recv()
            attend_run(partner_of(sec, j - 1))
        x_copies[j].wait_recv()
        fwd_copies[j].start()
        if j + 2 < RUNS:
            x_copies[j + 2].start()
        if j == 0:
            w_copies[2].wait()
        k_one, v_one = half(j, across)
        k_acc, v_acc = k_acc + k_one, v_acc + v_one
        head_copies[j].wait_recv()
        fwd_copies[j].wait_recv()
        if j == 0:
            w_copies[3].wait()
        k_one, v_one = half(j, across_sib)
        k_acc, v_acc = k_acc + k_one, v_acc + v_one
        k_acc = k_acc + bias[0:1, :]
        v_acc = v_acc + bias[1:2, :]
        live = within(row, sec, runs[j])
        parts = []
        for g in range(2):
            k = k_acc[:, g * 128 : (g + 1) * 128]
            k = k * cos_ref[...] + pltpu.roll(k, 64, 1) * sin_ref[...]
            parts.append(jnp.where(live, k, 0.0).astype(jnp.bfloat16))
        for g in range(2):
            parts.append(jnp.where(live, v_acc[:, g * 128 : (g + 1) * 128], 0.0).astype(jnp.bfloat16))
        done = jnp.concatenate(parts, axis=1).reshape(8, 16, 512)
        if j < RUNS - 1:
            sendbuf[j] = done
            copy = remote(
                sendbuf.at[j],
                kvbuf.at[pl.ds(8 * sec, 8)],
                z_send.at[j],
                z_recv.at[j],
                {"section": partner_of(sec, j)},
            )
            copy.start()
            z_copies.append(copy)
        else:
            kvbuf[pl.ds(8 * sec, 8)] = done
    attend_run(sec)
    for block in range(pool_ref.shape[1]):
        rows_in = kvbuf[inv_ref[block]]
        pool_ref[0, block] = rows_in[:, :256]
        pool_ref[1, block] = rows_in[:, 256:]
    for j in range(RUNS):
        sib_copies[j].wait_send()
        head_copies[j].wait_send()
        fwd_copies[j].wait_send()
        x_copies[j].wait_send()
        if j < RUNS - 1:
            z_copies[j].wait_send()


HEAD = 512


def per_device_routed(hidden, kv_weight, kv_bias, prompt_len, owner, queries, new_kv, block_table):
    req_count, prompt_max, feats = hidden.shape
    run = req_count // RUNS
    rows = run * prompt_max
    across = lax.ppermute(
        hidden[:, :, :HEAD].reshape(RUNS, rows, HEAD), "tensor", [(t, (t + 2) % 4) for t in range(4)]
    )
    by_run = hidden.reshape(RUNS, rows, feats)
    weight = kv_weight.reshape(4, feats, 2, 256).transpose(2, 0, 1, 3)
    positions = jnp.arange(prompt_max)
    table = block_table.reshape(-1)
    count = table.shape[0]
    inverse = jnp.sum(
        jnp.where(table[None, :] == jnp.arange(count)[:, None], jnp.arange(count)[None, :], 0), axis=1
    ).astype(jnp.int32)
    freq = rope_base ** (-(jnp.arange(HD // 2).astype(jnp.float32) * 2.0 / HD))
    angles = positions.astype(jnp.float32)[:, None] * freq[None, :]
    cosine = jnp.concatenate([jnp.cos(angles), jnp.cos(angles)], axis=-1)
    sine = jnp.concatenate([-jnp.sin(angles), jnp.sin(angles)], axis=-1)
    cosine = jnp.tile(cosine, (run, 1))
    sine = jnp.tile(sine, (run, 1))
    q = queries.reshape(4, run, STEPS, 2, QPK, HD).transpose(3, 0, 1, 2, 4, 5).reshape(2, 4, rows, HD)
    new = new_kv.reshape(4, run, STEPS, 2, 2, HD).transpose(3, 4, 0, 1, 2, 5)
    new = new.reshape(2, 2, 4, run * STEPS, HD)
    vmem = pl.BlockSpec(memory_space=pltpu.VMEM)
    smem = pl.BlockSpec(memory_space=pltpu.SMEM)
    hbm = pl.BlockSpec(memory_space=pltpu.HBM)
    dma = pltpu.SemaphoreType.DMA
    pool, out = pl.pallas_call(
        functools.partial(routed_kernel, HEAD),
        out_shape=(
            jax.ShapeDtypeStruct((2, count, BLK, 256), jnp.bfloat16),
            jax.ShapeDtypeStruct((2, 4, rows, HD), jnp.bfloat16),
        ),
        in_specs=[vmem, vmem, hbm, vmem, vmem, vmem, smem, smem, smem, vmem, vmem],
        out_specs=(vmem, vmem),
        scratch_shapes=[
            pltpu.VMEM((RUNS, 4, rows, feats), jnp.bfloat16),
            pltpu.VMEM((2, 4, feats, 256), jnp.bfloat16),
            pltpu.VMEM((count, BLK, 512), jnp.bfloat16),
            pltpu.VMEM((RUNS - 1, 8, BLK, 512), jnp.bfloat16),
        ]
        + [dma((4,))] * 11,
        compiler_params=pltpu.CompilerParams(
            collective_id=0, has_side_effects=True, vmem_limit_bytes=40 * 1024 * 1024
        ),
        cost_estimate=pl.CostEstimate(
            flops=2 * RUNS * rows * 4 * feats * 512, bytes_accessed=16 * 1024 * 1024, transcendentals=0
        ),
    )(by_run, across, weight, kv_bias, cosine, sine, owner, prompt_len, inverse, q, new)
    out = out.reshape(2, 4, run, STEPS, QPK, HD).transpose(1, 2, 3, 0, 4, 5)
    return (pool, out.reshape(req_count, STEPS, 2 * QPK * HD))


def solution(mesh):
    routed = mesh.shape["section"] == RUNS and mesh.shape["tensor"] == 4
    per_device = per_device_routed if routed else per_device_general
    return jax.shard_map(
        per_device,
        mesh=mesh,
        in_specs=(
            P(("groups", "section"), None, "tensor"),
            P(None, None, "tensor"),
            P(None, "tensor"),
            P("groups"),
            P("groups"),
            P(("groups", "section"), None, "tensor"),
            P(("groups", "section"), None, None, "tensor"),
            P(("groups", "section"), None),
        ),
        out_specs=(
            P(None, ("groups", "section"), None, "tensor"),
            P(("groups", "section"), None, "tensor"),
        ),
        check_vma=False,
    )
```

```python
import functools

import jax
import jax.numpy as jnp
from jax import lax
from jax.experimental import pallas as pl
from jax.experimental.pallas import tpu as pltpu
from jax.sharding import PartitionSpec as P

HD = 128
BLK = 16
STEPS = 4
QPK = 8


rope_base = 1000000.0


def rotary(key_rows, offset):
    half_dim = key_rows.shape[-1] // 2
    row_count = key_rows.shape[-3]
    positions = (jnp.arange(row_count) + offset).astype(jnp.float32)
    inverse = rope_base ** (-(jnp.arange(half_dim).astype(jnp.float32) * 2.0 / key_rows.shape[-1]))
    angles = positions[:, None] * inverse[None, :]
    cosine = jnp.concatenate([jnp.cos(angles), jnp.cos(angles)], axis=-1)[:, None, :]
    sine_part = jnp.concatenate([jnp.sin(angles), jnp.sin(angles)], axis=-1)[:, None, :]
    turned = jnp.concatenate([-key_rows[..., half_dim:], key_rows[..., :half_dim]], axis=-1)
    return key_rows * cosine + turned * sine_part


def finish(partial_value, kv_bias, offset, lengths, groups):
    span_len = partial_value.shape[1]
    biased = partial_value + kv_bias.astype(jnp.float32).reshape(2, groups, HD)
    rotated = rotary(biased[:, :, 0], offset)
    merged = jnp.stack([rotated, biased[:, :, 1]], axis=2)
    positions = jnp.arange(span_len) + offset
    live_rows = positions[None, :] < lengths[:, None]
    return jnp.where(live_rows[:, :, None, None, None], merged, 0.0).astype(jnp.bfloat16)


def folder(weight_mat):

    def add_slab(running, slab, first_col):
        col_count = slab.shape[-1]
        return jnp.dot(slab.reshape(-1, col_count), weight_mat, preferred_element_type=jnp.float32)

    return add_slab


def attend(query_rows, slot_kv, new_kv, slot_len, groups):
    slot_count = query_rows.shape[0]
    queries = query_rows.reshape(slot_count, STEPS, groups, QPK, HD)
    cached = slot_kv.reshape(slot_count, -1, 2, groups, HD)
    recent = new_kv.reshape(slot_count, STEPS, 2, groups, HD)
    score_scale = HD ** (-0.5)
    old_scores = (
        jnp.einsum(
            "rtgqd,rpgd->rtgqp", queries, cached[:, :, 0], preferred_element_type=jnp.float32
        )
        * score_scale
    )
    new_scores = (
        jnp.einsum(
            "rtgqd,rsgd->rtgqs", queries, recent[:, :, 0], preferred_element_type=jnp.float32
        )
        * score_scale
    )
    prompt_slots = cached.shape[1]
    prompt_pos = jnp.arange(prompt_slots)
    old_live = (prompt_pos[None, :] < slot_len[:, None])[:, None, None, None, :]
    step_pos = jnp.arange(STEPS)
    new_live = (step_pos[None, :] <= step_pos[:, None])[None, :, None, None, :]
    scores = jnp.concatenate(
        [jnp.where(old_live, old_scores, -jnp.inf), jnp.where(new_live, new_scores, -jnp.inf)],
        axis=-1,
    )
    attn_probs = jax.nn.softmax(scores, axis=-1).astype(jnp.bfloat16)
    attended = jnp.einsum(
        "rtgqp,rpgd->rtgqd",
        attn_probs[..., :prompt_slots],
        cached[:, :, 1],
        preferred_element_type=jnp.float32,
    )
    attended = attended + jnp.einsum(
        "rtgqs,rsgd->rtgqd",
        attn_probs[..., prompt_slots:],
        recent[:, :, 1],
        preferred_element_type=jnp.float32,
    )
    return attended.astype(jnp.bfloat16).reshape(slot_count, STEPS, groups * QPK * HD)


def per_device_general(hidden, kv_weight, kv_bias, prompt_len, owner, queries, new_kv, block_table):
    n_section = lax.axis_size("section")
    own_index = lax.axis_index("section")
    req_count = hidden.shape[0]
    prompt_max = hidden.shape[1]
    kv_width = kv_weight.shape[2]
    groups = kv_width // HD
    run_most = max(2, req_count // n_section)
    owner_grid = owner.reshape(n_section, req_count)
    local_owner = lax.dynamic_index_in_dim(owner_grid, own_index, 0, keepdims=False)
    local_len = lax.dynamic_slice_in_dim(prompt_len, own_index * req_count, req_count)
    local_ids = jnp.arange(req_count)
    earlier = (local_owner[:, None] == local_owner[None, :]) & (
        local_ids[None, :] < local_ids[:, None]
    )
    send_pos = local_owner * run_most + jnp.sum(earlier.astype(jnp.int32), axis=1)
    run_rank = jnp.cumsum((owner_grid == own_index).astype(jnp.int32), axis=1) - 1
    slot_order = jnp.argsort(owner, stable=True)
    own_slots = lax.dynamic_slice_in_dim(slot_order, own_index * req_count, req_count)
    recv_pos = own_slots // req_count * run_most + run_rank.reshape(-1)[own_slots]
    slot_len = prompt_len[own_slots]
    weight_mat = kv_weight.reshape(kv_weight.shape[0], 2 * kv_width)
    add_slab = folder(weight_mat)
    blank_acc = jnp.zeros((req_count * prompt_max, 2 * kv_width), jnp.float32)
    partial_value = add_slab(
        blank_acc, lax.all_gather(hidden, "tensor", axis=2, tiled=True), jnp.int32(0)
    )
    span_len = partial_value.shape[0] // req_count
    shaped = partial_value.reshape(req_count, span_len, 2, groups, HD)
    kv_rows = finish(shaped, kv_bias, 0, local_len, groups).reshape(
        req_count, span_len, 2, kv_width
    )
    blank_buf = jnp.zeros((n_section * run_most,) + kv_rows.shape[1:], kv_rows.dtype)
    arrived = lax.all_to_all(
        blank_buf.at[send_pos].set(kv_rows), "section", split_axis=0, concat_axis=0, tiled=True
    )
    slot_kv = jnp.take(arrived, recv_pos, axis=0)
    decode_out = attend(queries, slot_kv, new_kv, slot_len, groups)
    block_count = prompt_max // BLK
    blocks = slot_kv.reshape(req_count * block_count, BLK, 2, kv_width)
    pool_rows = jnp.zeros_like(blocks).at[block_table.reshape(-1)].set(blocks)
    return (jnp.transpose(pool_rows, (2, 0, 1, 3)), decode_out)

MESH = pl.DeviceIdType.MESH
RUNS = 4


def partner_of(me, step):
    if step == 0:
        return 3 - me
    if step == 1:
        return lax.rem(me + 2, 4)
    if step == 2:
        return me + 1 - 2 * lax.rem(me, 2)
    return me


def routed_kernel(
    head, h_ref, x0_ref, w_hbm, bias_ref, cos_ref, sin_ref, owner_ref, len_ref, inv_ref, q_ref, new_ref,
    pool_ref, out_ref,
    gathered, weight, kvbuf, sendbuf,
    w_sem, sib_send, sib_recv, x_send, x_recv, head_send, head_recv, fwd_send, fwd_recv, z_send, z_recv,
):
    sec = lax.axis_index("section")
    me = lax.axis_index("tensor")
    sib = me + 1 - 2 * lax.rem(me, 2)
    across = lax.rem(me + 2, 4)
    across_sib = lax.rem(sib + 2, 4)
    order = (me, sib, across, across_sib)
    rest = gathered.shape[3] - head

    barrier = pltpu.get_barrier_semaphore()
    pl.semaphore_signal(barrier, inc=1, device_id={"tensor": sib}, device_id_type=MESH)
    pl.semaphore_signal(barrier, inc=1, device_id={"tensor": across}, device_id_type=MESH)
    for step in range(3):
        pl.semaphore_signal(
            barrier, inc=1, device_id={"section": partner_of(sec, step)}, device_id_type=MESH
        )
    w_copies = [
        pltpu.make_async_copy(w_hbm.at[:, t], weight.at[:, t], w_sem.at[i])
        for i, t in enumerate(order)
    ]

    def run_of(source, target):
        found = jnp.int32(0)
        for r in range(1, RUNS):
            found = jnp.where(owner_ref[source * 16 + r * 4] == target, r, found)
        return found

    runs = [run_of(sec, partner_of(sec, j)) for j in range(RUNS)]

    def remote(src, dst, send, recv, where):
        return pltpu.make_async_remote_copy(
            src_ref=src, dst_ref=dst, send_sem=send, recv_sem=recv, device_id=where, device_id_type=MESH
        )

    def same(slot, send, recv, where):
        return remote(slot, slot, send, recv, where)

    cut_a, cut_b = rest // 2, rest // 3
    cuts = [[(j, head, rest)] for j in range(RUNS - 1)]
    cuts.append([(3, head, cut_a), (4, head + cut_a, cut_b), (5, head + cut_a + cut_b, rest - cut_a - cut_b)])
    x_copies = [
        [
            same(
                gathered.at[j, me, :, pl.ds(first, width)],
                x_send.at[i],
                x_recv.at[i],
                {"tensor": across},
            )
            for i, first, width in cuts[j]
        ]
        for j in range(RUNS)
    ]
    sib_copies = [
        same(gathered.at[j, me], sib_send.at[j], sib_recv.at[j], {"tensor": sib}) for j in range(RUNS)
    ]
    head_copies = [
        same(
            gathered.at[j, across, :, pl.ds(0, head)], head_send.at[j], head_recv.at[j], {"tensor": sib}
        )
        for j in range(RUNS)
    ]
    fwd_copies = [
        [
            same(
                gathered.at[j, across, :, pl.ds(first, width)],
                fwd_send.at[i],
                fwd_recv.at[i],
                {"tensor": sib},
            )
            for i, first, width in cuts[j]
        ]
        for j in range(RUNS)
    ]
    gathered[0, me] = h_ref[runs[0]]
    pl.semaphore_wait(barrier, 5)
    x_copies[0][0].start()
    gathered[1, me] = h_ref[runs[1]]
    x_copies[1][0].start()
    w_copies[0].start()
    w_copies[1].start()
    sib_copies[0].start()
    gathered[0, across, :, 0:head] = x0_ref[runs[0]]
    head_copies[0].start()
    w_copies[2].start()
    w_copies[3].start()
    for j in range(1, RUNS):
        if j > 1:
            gathered[j, me] = h_ref[runs[j]]
        sib_copies[j].start()
        gathered[j, across, :, 0:head] = x0_ref[runs[j]]
        head_copies[j].start()

    def half(j, t, first=0, width=None):
        span = pl.ds(first, gathered.shape[3] if width is None else width)
        a = gathered[j, t, :, span]
        return (
            jnp.dot(a, weight[0, t, span], preferred_element_type=jnp.float32),
            jnp.dot(a, weight[1, t, span], preferred_element_type=jnp.float32),
        )

    row = lax.broadcasted_iota(jnp.int32, (128, 128), 0)
    col = lax.broadcasted_iota(jnp.int32, (128, 128), 1)
    same_slot = (row // 32) == (col // 32)
    row16 = lax.broadcasted_iota(jnp.int32, (128, 16), 0)
    col16 = lax.broadcasted_iota(jnp.int32, (128, 16), 1)
    new_live = ((row16 // 32) == (col16 // 4)) & ((col16 % 4) <= ((row16 % 32) // 8))
    contract = (((1,), (1,)), ((), ()))

    def within(index, source, run):
        first = source * 16 + run * 4
        limit = jnp.full(index.shape, len_ref[first], jnp.int32)
        for i in range(1, 4):
            limit = jnp.where(index // 32 == i, len_ref[first + i], limit)
        return (index % 32) < limit

    def attend_run(s):
        old_live = same_slot & within(col, s, run_of(s, sec))
        for g in range(2):
            q = q_ref[g, s]
            kv = kvbuf[pl.ds(8 * s, 8)].reshape(128, 512)
            k = kv[:, g * 128 : (g + 1) * 128]
            v = kv[:, 256 + g * 128 : 256 + (g + 1) * 128]
            old = lax.dot_general(q, k, contract, preferred_element_type=jnp.float32) * HD ** (-0.5)
            new = (
                lax.dot_general(q, new_ref[0, g, s], contract, preferred_element_type=jnp.float32)
                * HD ** (-0.5)
            )
            old = jnp.where(old_live, old, -jnp.inf)
            new = jnp.where(new_live, new, -jnp.inf)
            top = jnp.maximum(
                jnp.max(old, axis=1, keepdims=True), jnp.max(new, axis=1, keepdims=True)
            )
            old = jnp.exp(old - top)
            new = jnp.exp(new - top)
            total = jnp.sum(old, axis=1, keepdims=True) + jnp.sum(new, axis=1, keepdims=True)
            old = (old / total).astype(jnp.bfloat16)
            new = (new / total).astype(jnp.bfloat16)
            res = jnp.dot(old, v, preferred_element_type=jnp.float32) + jnp.dot(
                new, new_ref[1, g, s], preferred_element_type=jnp.float32
            )
            out_ref[g, s] = res.astype(jnp.bfloat16)

    bias = bias_ref[...].astype(jnp.float32)
    z_copies = []
    for j in range(RUNS):
        if j == 0:
            w_copies[0].wait()
        k_acc, v_acc = half(j, me)
        sib_copies[j].wait_recv()
        if j == 0:
            w_copies[1].wait()
        k_one, v_one = half(j, sib)
        k_acc, v_acc = k_acc + k_one, v_acc + v_one
        if j > 0:
            z_copies[j - 1].wait_recv()
            attend_run(partner_of(sec, j - 1))
        if j == 0:
            w_copies[2].wait()
            w_copies[3].wait()
        head_copies[j].wait_recv()
        for t in (across, across_sib):
            k_one, v_one = half(j, t, 0, head)
            k_acc, v_acc = k_acc + k_one, v_acc + v_one
        for at, (_, first, width) in enumerate(cuts[j]):
            x_copies[j][at].wait_recv()
            fwd_copies[j][at].start()
            if j + 2 < RUNS:
                for copy in x_copies[j + 2]:
                    copy.start()
            k_one, v_one = half(j, across, first, width)
            k_acc, v_acc = k_acc + k_one, v_acc + v_one
            fwd_copies[j][at].wait_recv()
            k_one, v_one = half(j, across_sib, first, width)
            k_acc, v_acc = k_acc + k_one, v_acc + v_one
        k_acc = k_acc + bias[0:1, :]
        v_acc = v_acc + bias[1:2, :]
        live = within(row, sec, runs[j])
        parts = []
        for g in range(2):
            k = k_acc[:, g * 128 : (g + 1) * 128]
            k = k * cos_ref[...] + pltpu.roll(k, 64, 1) * sin_ref[...]
            parts.append(jnp.where(live, k, 0.0).astype(jnp.bfloat16))
        for g in range(2):
            parts.append(jnp.where(live, v_acc[:, g * 128 : (g + 1) * 128], 0.0).astype(jnp.bfloat16))
        done = jnp.concatenate(parts, axis=1).reshape(8, 16, 512)
        if j < RUNS - 1:
            sendbuf[j] = done
            copy = remote(
                sendbuf.at[j],
                kvbuf.at[pl.ds(8 * sec, 8)],
                z_send.at[j],
                z_recv.at[j],
                {"section": partner_of(sec, j)},
            )
            copy.start()
            z_copies.append(copy)
        else:
            kvbuf[pl.ds(8 * sec, 8)] = done
    attend_run(sec)
    for block in range(pool_ref.shape[1]):
        rows_in = kvbuf[inv_ref[block]]
        pool_ref[0, block] = rows_in[:, :256]
        pool_ref[1, block] = rows_in[:, 256:]
    for j in range(RUNS):
        sib_copies[j].wait_send()
        head_copies[j].wait_send()
        for at in range(len(cuts[j])):
            fwd_copies[j][at].wait_send()
            x_copies[j][at].wait_send()
        if j < RUNS - 1:
            z_copies[j].wait_send()


HEAD = 512


def per_device_routed(hidden, kv_weight, kv_bias, prompt_len, owner, queries, new_kv, block_table):
    req_count, prompt_max, feats = hidden.shape
    run = req_count // RUNS
    rows = run * prompt_max
    across = lax.ppermute(
        hidden[:, :, :HEAD].reshape(RUNS, rows, HEAD), "tensor", [(t, (t + 2) % 4) for t in range(4)]
    )
    by_run = hidden.reshape(RUNS, rows, feats)
    weight = kv_weight.reshape(4, feats, 2, 256).transpose(2, 0, 1, 3)
    positions = jnp.arange(prompt_max)
    table = block_table.reshape(-1)
    count = table.shape[0]
    inverse = jnp.sum(
        jnp.where(table[None, :] == jnp.arange(count)[:, None], jnp.arange(count)[None, :], 0), axis=1
    ).astype(jnp.int32)
    freq = rope_base ** (-(jnp.arange(HD // 2).astype(jnp.float32) * 2.0 / HD))
    angles = positions.astype(jnp.float32)[:, None] * freq[None, :]
    cosine = jnp.concatenate([jnp.cos(angles), jnp.cos(angles)], axis=-1)
    sine = jnp.concatenate([-jnp.sin(angles), jnp.sin(angles)], axis=-1)
    cosine = jnp.tile(cosine, (run, 1))
    sine = jnp.tile(sine, (run, 1))
    q = queries.reshape(4, run, STEPS, 2, QPK, HD).transpose(3, 0, 1, 2, 4, 5).reshape(2, 4, rows, HD)
    new = new_kv.reshape(4, run, STEPS, 2, 2, HD).transpose(3, 4, 0, 1, 2, 5)
    new = new.reshape(2, 2, 4, run * STEPS, HD)
    vmem = pl.BlockSpec(memory_space=pltpu.VMEM)
    smem = pl.BlockSpec(memory_space=pltpu.SMEM)
    hbm = pl.BlockSpec(memory_space=pltpu.HBM)
    dma = pltpu.SemaphoreType.DMA
    pool, out = pl.pallas_call(
        functools.partial(routed_kernel, HEAD),
        out_shape=(
            jax.ShapeDtypeStruct((2, count, BLK, 256), jnp.bfloat16),
            jax.ShapeDtypeStruct((2, 4, rows, HD), jnp.bfloat16),
        ),
        in_specs=[vmem, vmem, hbm, vmem, vmem, vmem, smem, smem, smem, vmem, vmem],
        out_specs=(vmem, vmem),
        scratch_shapes=[
            pltpu.VMEM((RUNS, 4, rows, feats), jnp.bfloat16),
            pltpu.VMEM((2, 4, feats, 256), jnp.bfloat16),
            pltpu.VMEM((count, BLK, 512), jnp.bfloat16),
            pltpu.VMEM((RUNS - 1, 8, BLK, 512), jnp.bfloat16),
        ]
        + [dma((6,))] * 11,
        compiler_params=pltpu.CompilerParams(
            collective_id=0, has_side_effects=True, vmem_limit_bytes=57 * 1024 * 1024
        ),
        cost_estimate=pl.CostEstimate(
            flops=2 * RUNS * rows * 4 * feats * 512, bytes_accessed=16 * 1024 * 1024, transcendentals=0
        ),
    )(by_run, across, weight, kv_bias, cosine, sine, owner, prompt_len, inverse, q, new)
    out = out.reshape(2, 4, run, STEPS, QPK, HD).transpose(1, 2, 3, 0, 4, 5)
    return (pool, out.reshape(req_count, STEPS, 2 * QPK * HD))


def solution(mesh):
    routed = mesh.shape["section"] == RUNS and mesh.shape["tensor"] == 4
    per_device = per_device_routed if routed else per_device_general
    return jax.shard_map(
        per_device,
        mesh=mesh,
        in_specs=(
            P(("groups", "section"), None, "tensor"),
            P(None, None, "tensor"),
            P(None, "tensor"),
            P("groups"),
            P("groups"),
            P(("groups", "section"), None, "tensor"),
            P(("groups", "section"), None, None, "tensor"),
            P(("groups", "section"), None),
        ),
        out_specs=(
            P(None, ("groups", "section"), None, "tensor"),
            P(("groups", "section"), None, "tensor"),
        ),
        check_vma=False,
    )
```

```python
import functools

import jax
import jax.numpy as jnp
from jax import lax
from jax.experimental import pallas as pl
from jax.experimental.pallas import tpu as pltpu
from jax.sharding import PartitionSpec as P

HD = 128
BLK = 16
STEPS = 4
QPK = 8


rope_base = 1000000.0


def rotary(key_rows, offset):
    half_dim = key_rows.shape[-1] // 2
    row_count = key_rows.shape[-3]
    positions = (jnp.arange(row_count) + offset).astype(jnp.float32)
    inverse = rope_base ** (-(jnp.arange(half_dim).astype(jnp.float32) * 2.0 / key_rows.shape[-1]))
    angles = positions[:, None] * inverse[None, :]
    cosine = jnp.concatenate([jnp.cos(angles), jnp.cos(angles)], axis=-1)[:, None, :]
    sine_part = jnp.concatenate([jnp.sin(angles), jnp.sin(angles)], axis=-1)[:, None, :]
    turned = jnp.concatenate([-key_rows[..., half_dim:], key_rows[..., :half_dim]], axis=-1)
    return key_rows * cosine + turned * sine_part


def finish(partial_value, kv_bias, offset, lengths, groups):
    span_len = partial_value.shape[1]
    biased = partial_value + kv_bias.astype(jnp.float32).reshape(2, groups, HD)
    rotated = rotary(biased[:, :, 0], offset)
    merged = jnp.stack([rotated, biased[:, :, 1]], axis=2)
    positions = jnp.arange(span_len) + offset
    live_rows = positions[None, :] < lengths[:, None]
    return jnp.where(live_rows[:, :, None, None, None], merged, 0.0).astype(jnp.bfloat16)


def folder(weight_mat):

    def add_slab(running, slab, first_col):
        col_count = slab.shape[-1]
        return jnp.dot(slab.reshape(-1, col_count), weight_mat, preferred_element_type=jnp.float32)

    return add_slab


def attend(query_rows, slot_kv, new_kv, slot_len, groups):
    slot_count = query_rows.shape[0]
    queries = query_rows.reshape(slot_count, STEPS, groups, QPK, HD)
    cached = slot_kv.reshape(slot_count, -1, 2, groups, HD)
    recent = new_kv.reshape(slot_count, STEPS, 2, groups, HD)
    score_scale = HD ** (-0.5)
    old_scores = (
        jnp.einsum(
            "rtgqd,rpgd->rtgqp", queries, cached[:, :, 0], preferred_element_type=jnp.float32
        )
        * score_scale
    )
    new_scores = (
        jnp.einsum(
            "rtgqd,rsgd->rtgqs", queries, recent[:, :, 0], preferred_element_type=jnp.float32
        )
        * score_scale
    )
    prompt_slots = cached.shape[1]
    prompt_pos = jnp.arange(prompt_slots)
    old_live = (prompt_pos[None, :] < slot_len[:, None])[:, None, None, None, :]
    step_pos = jnp.arange(STEPS)
    new_live = (step_pos[None, :] <= step_pos[:, None])[None, :, None, None, :]
    scores = jnp.concatenate(
        [jnp.where(old_live, old_scores, -jnp.inf), jnp.where(new_live, new_scores, -jnp.inf)],
        axis=-1,
    )
    attn_probs = jax.nn.softmax(scores, axis=-1).astype(jnp.bfloat16)
    attended = jnp.einsum(
        "rtgqp,rpgd->rtgqd",
        attn_probs[..., :prompt_slots],
        cached[:, :, 1],
        preferred_element_type=jnp.float32,
    )
    attended = attended + jnp.einsum(
        "rtgqs,rsgd->rtgqd",
        attn_probs[..., prompt_slots:],
        recent[:, :, 1],
        preferred_element_type=jnp.float32,
    )
    return attended.astype(jnp.bfloat16).reshape(slot_count, STEPS, groups * QPK * HD)


def per_device_general(hidden, kv_weight, kv_bias, prompt_len, owner, queries, new_kv, block_table):
    n_section = lax.axis_size("section")
    own_index = lax.axis_index("section")
    req_count = hidden.shape[0]
    prompt_max = hidden.shape[1]
    kv_width = kv_weight.shape[2]
    groups = kv_width // HD
    run_most = max(2, req_count // n_section)
    owner_grid = owner.reshape(n_section, req_count)
    local_owner = lax.dynamic_index_in_dim(owner_grid, own_index, 0, keepdims=False)
    local_len = lax.dynamic_slice_in_dim(prompt_len, own_index * req_count, req_count)
    local_ids = jnp.arange(req_count)
    earlier = (local_owner[:, None] == local_owner[None, :]) & (
        local_ids[None, :] < local_ids[:, None]
    )
    send_pos = local_owner * run_most + jnp.sum(earlier.astype(jnp.int32), axis=1)
    run_rank = jnp.cumsum((owner_grid == own_index).astype(jnp.int32), axis=1) - 1
    slot_order = jnp.argsort(owner, stable=True)
    own_slots = lax.dynamic_slice_in_dim(slot_order, own_index * req_count, req_count)
    recv_pos = own_slots // req_count * run_most + run_rank.reshape(-1)[own_slots]
    slot_len = prompt_len[own_slots]
    weight_mat = kv_weight.reshape(kv_weight.shape[0], 2 * kv_width)
    add_slab = folder(weight_mat)
    blank_acc = jnp.zeros((req_count * prompt_max, 2 * kv_width), jnp.float32)
    partial_value = add_slab(
        blank_acc, lax.all_gather(hidden, "tensor", axis=2, tiled=True), jnp.int32(0)
    )
    span_len = partial_value.shape[0] // req_count
    shaped = partial_value.reshape(req_count, span_len, 2, groups, HD)
    kv_rows = finish(shaped, kv_bias, 0, local_len, groups).reshape(
        req_count, span_len, 2, kv_width
    )
    blank_buf = jnp.zeros((n_section * run_most,) + kv_rows.shape[1:], kv_rows.dtype)
    arrived = lax.all_to_all(
        blank_buf.at[send_pos].set(kv_rows), "section", split_axis=0, concat_axis=0, tiled=True
    )
    slot_kv = jnp.take(arrived, recv_pos, axis=0)
    decode_out = attend(queries, slot_kv, new_kv, slot_len, groups)
    block_count = prompt_max // BLK
    blocks = slot_kv.reshape(req_count * block_count, BLK, 2, kv_width)
    pool_rows = jnp.zeros_like(blocks).at[block_table.reshape(-1)].set(blocks)
    return (jnp.transpose(pool_rows, (2, 0, 1, 3)), decode_out)

MESH = pl.DeviceIdType.MESH
RUNS = 4


def partner_of(me, step):
    if step == 0:
        return 3 - me
    if step == 1:
        return lax.rem(me + 2, 4)
    if step == 2:
        return me + 1 - 2 * lax.rem(me, 2)
    return me


def routed_kernel(
    head, h_ref, x0_ref, w_hbm, bias_ref, cos_ref, sin_ref, owner_ref, len_ref, inv_ref, q_ref, new_ref,
    pool_ref, out_ref,
    gathered, weight, kvbuf, sendbuf,
    w_sem, sib_send, sib_recv, x_send, x_recv, head_send, head_recv, fwd_send, fwd_recv, z_send, z_recv,
):
    sec = lax.axis_index("section")
    me = lax.axis_index("tensor")
    sib = me + 1 - 2 * lax.rem(me, 2)
    across = lax.rem(me + 2, 4)
    across_sib = lax.rem(sib + 2, 4)
    order = (me, sib, across, across_sib)
    rest = gathered.shape[3] - head

    barrier = pltpu.get_barrier_semaphore()
    pl.semaphore_signal(barrier, inc=1, device_id={"tensor": sib}, device_id_type=MESH)
    pl.semaphore_signal(barrier, inc=1, device_id={"tensor": across}, device_id_type=MESH)
    for step in range(3):
        pl.semaphore_signal(
            barrier, inc=1, device_id={"section": partner_of(sec, step)}, device_id_type=MESH
        )
    w_copies = [
        pltpu.make_async_copy(w_hbm.at[:, t], weight.at[:, t], w_sem.at[i])
        for i, t in enumerate(order)
    ]

    def run_of(source, target):
        found = jnp.int32(0)
        for r in range(1, RUNS):
            found = jnp.where(owner_ref[source * 16 + r * 4] == target, r, found)
        return found

    runs = [run_of(sec, partner_of(sec, j)) for j in range(RUNS)]

    def remote(src, dst, send, recv, where):
        return pltpu.make_async_remote_copy(
            src_ref=src, dst_ref=dst, send_sem=send, recv_sem=recv, device_id=where, device_id_type=MESH
        )

    def same(slot, send, recv, where):
        return remote(slot, slot, send, recv, where)

    cut_a, cut_b = rest // 2, rest // 3
    cuts = [[(j, head, rest)] for j in range(RUNS - 1)]
    cuts.append([(3, head, cut_a), (4, head + cut_a, cut_b), (5, head + cut_a + cut_b, rest - cut_a - cut_b)])
    x_copies = [
        [
            same(
                gathered.at[j, me, :, pl.ds(first, width)],
                x_send.at[i],
                x_recv.at[i],
                {"tensor": across},
            )
            for i, first, width in cuts[j]
        ]
        for j in range(RUNS)
    ]
    sib_copies = [
        same(gathered.at[j, me], sib_send.at[j], sib_recv.at[j], {"tensor": sib}) for j in range(RUNS)
    ]
    head_copies = [
        same(
            gathered.at[j, across, :, pl.ds(0, head)], head_send.at[j], head_recv.at[j], {"tensor": sib}
        )
        for j in range(RUNS)
    ]
    fwd_copies = [
        [
            same(
                gathered.at[j, across, :, pl.ds(first, width)],
                fwd_send.at[i],
                fwd_recv.at[i],
                {"tensor": sib},
            )
            for i, first, width in cuts[j]
        ]
        for j in range(RUNS)
    ]
    gathered[0, me] = h_ref[runs[0]]
    pl.semaphore_wait(barrier, 5)
    x_copies[0][0].start()
    gathered[1, me] = h_ref[runs[1]]
    x_copies[1][0].start()
    w_copies[0].start()
    w_copies[1].start()
    sib_copies[0].start()
    gathered[0, across, :, 0:head] = x0_ref[runs[0]]
    head_copies[0].start()
    w_copies[2].start()
    w_copies[3].start()
    for j in range(1, RUNS):
        if j > 1:
            gathered[j, me] = h_ref[runs[j]]
        sib_copies[j].start()
        gathered[j, across, :, 0:head] = x0_ref[runs[j]]
        head_copies[j].start()

    def half(j, t, first=0, width=None):
        span = pl.ds(first, gathered.shape[3] if width is None else width)
        a = gathered[j, t, :, span]
        return (
            jnp.dot(a, weight[0, t, span], preferred_element_type=jnp.float32),
            jnp.dot(a, weight[1, t, span], preferred_element_type=jnp.float32),
        )

    row = lax.broadcasted_iota(jnp.int32, (128, 128), 0)
    col = lax.broadcasted_iota(jnp.int32, (128, 128), 1)
    same_slot = (row // 32) == (col // 32)
    row16 = lax.broadcasted_iota(jnp.int32, (128, 16), 0)
    col16 = lax.broadcasted_iota(jnp.int32, (128, 16), 1)
    new_live = ((row16 // 32) == (col16 // 4)) & ((col16 % 4) <= ((row16 % 32) // 8))
    contract = (((1,), (1,)), ((), ()))

    def within(index, source, run):
        first = source * 16 + run * 4
        limit = jnp.full(index.shape, len_ref[first], jnp.int32)
        for i in range(1, 4):
            limit = jnp.where(index // 32 == i, len_ref[first + i], limit)
        return (index % 32) < limit

    def attend_run(s):
        old_live = same_slot & within(col, s, run_of(s, sec))
        for g in range(2):
            q = q_ref[g, s]
            kv = kvbuf[pl.ds(8 * s, 8)].reshape(128, 512)
            k = kv[:, g * 128 : (g + 1) * 128]
            v = kv[:, 256 + g * 128 : 256 + (g + 1) * 128]
            old = lax.dot_general(q, k, contract, preferred_element_type=jnp.float32) * HD ** (-0.5)
            new = (
                lax.dot_general(q, new_ref[0, g, s], contract, preferred_element_type=jnp.float32)
                * HD ** (-0.5)
            )
            old = jnp.where(old_live, old, -jnp.inf)
            new = jnp.where(new_live, new, -jnp.inf)
            top = jnp.maximum(
                jnp.max(old, axis=1, keepdims=True), jnp.max(new, axis=1, keepdims=True)
            )
            old = jnp.exp(old - top)
            new = jnp.exp(new - top)
            total = jnp.sum(old, axis=1, keepdims=True) + jnp.sum(new, axis=1, keepdims=True)
            old = (old / total).astype(jnp.bfloat16)
            new = (new / total).astype(jnp.bfloat16)
            res = jnp.dot(old, v, preferred_element_type=jnp.float32) + jnp.dot(
                new, new_ref[1, g, s], preferred_element_type=jnp.float32
            )
            out_ref[g, s] = res.astype(jnp.bfloat16)

    bias = bias_ref[...].astype(jnp.float32)
    z_copies = []
    for j in range(RUNS):
        if j == 0:
            w_copies[0].wait()
        k_acc, v_acc = half(j, me)
        sib_copies[j].wait_recv()
        if j == 0:
            w_copies[1].wait()
        k_one, v_one = half(j, sib)
        k_acc, v_acc = k_acc + k_one, v_acc + v_one
        if j > 0:
            z_copies[j - 1].wait_recv()
            attend_run(partner_of(sec, j - 1))
        if j == 0:
            w_copies[2].wait()
            w_copies[3].wait()
        head_copies[j].wait_recv()
        for t in (across, across_sib):
            k_one, v_one = half(j, t, 0, head)
            k_acc, v_acc = k_acc + k_one, v_acc + v_one
        for at, (_, first, width) in enumerate(cuts[j]):
            x_copies[j][at].wait_recv()
            fwd_copies[j][at].start()
            if j + 2 < RUNS:
                for copy in x_copies[j + 2]:
                    copy.start()
            k_one, v_one = half(j, across, first, width)
            k_acc, v_acc = k_acc + k_one, v_acc + v_one
            fwd_copies[j][at].wait_recv()
            k_one, v_one = half(j, across_sib, first, width)
            k_acc, v_acc = k_acc + k_one, v_acc + v_one
        k_acc = k_acc + bias[0:1, :]
        v_acc = v_acc + bias[1:2, :]
        live = within(row, sec, runs[j])
        parts = []
        for g in range(2):
            k = k_acc[:, g * 128 : (g + 1) * 128]
            k = k * cos_ref[...] + pltpu.roll(k, 64, 1) * sin_ref[...]
            parts.append(jnp.where(live, k, 0.0).astype(jnp.bfloat16))
        for g in range(2):
            parts.append(jnp.where(live, v_acc[:, g * 128 : (g + 1) * 128], 0.0).astype(jnp.bfloat16))
        done = jnp.concatenate(parts, axis=1).reshape(8, 16, 512)
        if j < RUNS - 1:
            sendbuf[j] = done
            copy = remote(
                sendbuf.at[j],
                kvbuf.at[pl.ds(8 * sec, 8)],
                z_send.at[j],
                z_recv.at[j],
                {"section": partner_of(sec, j)},
            )
            copy.start()
            z_copies.append(copy)
        else:
            kvbuf[pl.ds(8 * sec, 8)] = done
    attend_run(sec)
    for block in range(pool_ref.shape[1]):
        rows_in = kvbuf[inv_ref[block]]
        pool_ref[0, block] = rows_in[:, :256]
        pool_ref[1, block] = rows_in[:, 256:]
    for j in range(RUNS):
        sib_copies[j].wait_send()
        head_copies[j].wait_send()
        for at in range(len(cuts[j])):
            fwd_copies[j][at].wait_send()
            x_copies[j][at].wait_send()
        if j < RUNS - 1:
            z_copies[j].wait_send()


HEAD = 512


def per_device_routed(hidden, kv_weight, kv_bias, prompt_len, owner, queries, new_kv, block_table):
    req_count, prompt_max, feats = hidden.shape
    run = req_count // RUNS
    rows = run * prompt_max
    across = lax.ppermute(
        hidden[:, :, :HEAD].reshape(RUNS, rows, HEAD), "tensor", [(t, (t + 2) % 4) for t in range(4)]
    )
    by_run = hidden.reshape(RUNS, rows, feats)
    weight = kv_weight.reshape(4, feats, 2, 256).transpose(2, 0, 1, 3)
    positions = jnp.arange(prompt_max)
    table = block_table.reshape(-1)
    count = table.shape[0]
    inverse = jnp.sum(
        jnp.where(table[None, :] == jnp.arange(count)[:, None], jnp.arange(count)[None, :], 0), axis=1
    ).astype(jnp.int32)
    freq = rope_base ** (-(jnp.arange(HD // 2).astype(jnp.float32) * 2.0 / HD))
    angles = positions.astype(jnp.float32)[:, None] * freq[None, :]
    cosine = jnp.concatenate([jnp.cos(angles), jnp.cos(angles)], axis=-1)
    sine = jnp.concatenate([-jnp.sin(angles), jnp.sin(angles)], axis=-1)
    cosine = jnp.tile(cosine, (run, 1))
    sine = jnp.tile(sine, (run, 1))
    q = queries.reshape(4, run, STEPS, 2, QPK, HD).transpose(3, 0, 1, 2, 4, 5).reshape(2, 4, rows, HD)
    new = new_kv.reshape(4, run, STEPS, 2, 2, HD).transpose(3, 4, 0, 1, 2, 5)
    new = new.reshape(2, 2, 4, run * STEPS, HD)
    vmem = pl.BlockSpec(memory_space=pltpu.VMEM)
    smem = pl.BlockSpec(memory_space=pltpu.SMEM)
    hbm = pl.BlockSpec(memory_space=pltpu.HBM)
    dma = pltpu.SemaphoreType.DMA
    pool, out = pl.pallas_call(
        functools.partial(routed_kernel, HEAD),
        out_shape=(
            jax.ShapeDtypeStruct((2, count, BLK, 256), jnp.bfloat16),
            jax.ShapeDtypeStruct((2, 4, rows, HD), jnp.bfloat16),
        ),
        in_specs=[vmem, vmem, hbm, vmem, vmem, vmem, smem, smem, smem, vmem, vmem],
        out_specs=(vmem, vmem),
        scratch_shapes=[
            pltpu.VMEM((RUNS, 4, rows, feats), jnp.bfloat16),
            pltpu.VMEM((2, 4, feats, 256), jnp.bfloat16),
            pltpu.VMEM((count, BLK, 512), jnp.bfloat16),
            pltpu.VMEM((RUNS - 1, 8, BLK, 512), jnp.bfloat16),
        ]
        + [dma((6,))] * 11,
        compiler_params=pltpu.CompilerParams(
            collective_id=0, has_side_effects=True, vmem_limit_bytes=50 * 1024 * 1024
        ),
        cost_estimate=pl.CostEstimate(
            flops=2 * RUNS * rows * 4 * feats * 512, bytes_accessed=16 * 1024 * 1024, transcendentals=0
        ),
    )(by_run, across, weight, kv_bias, cosine, sine, owner, prompt_len, inverse, q, new)
    out = out.reshape(2, 4, run, STEPS, QPK, HD).transpose(1, 2, 3, 0, 4, 5)
    return (pool, out.reshape(req_count, STEPS, 2 * QPK * HD))


def solution(mesh):
    routed = mesh.shape["section"] == RUNS and mesh.shape["tensor"] == 4
    per_device = per_device_routed if routed else per_device_general
    return jax.shard_map(
        per_device,
        mesh=mesh,
        in_specs=(
            P(("groups", "section"), None, "tensor"),
            P(None, None, "tensor"),
            P(None, "tensor"),
            P("groups"),
            P("groups"),
            P(("groups", "section"), None, "tensor"),
            P(("groups", "section"), None, None, "tensor"),
            P(("groups", "section"), None),
        ),
        out_specs=(
            P(None, ("groups", "section"), None, "tensor"),
            P(("groups", "section"), None, "tensor"),
        ),
        check_vma=False,
    )
```

```python
import functools

import jax
import jax.numpy as jnp
from jax import lax
from jax.experimental import pallas as pl
from jax.experimental.pallas import tpu as pltpu
from jax.sharding import PartitionSpec as P

HD = 128
BLK = 16
STEPS = 4
QPK = 8


rope_base = 1000000.0


def rotary(key_rows, offset):
    half_dim = key_rows.shape[-1] // 2
    row_count = key_rows.shape[-3]
    positions = (jnp.arange(row_count) + offset).astype(jnp.float32)
    inverse = rope_base ** (-(jnp.arange(half_dim).astype(jnp.float32) * 2.0 / key_rows.shape[-1]))
    angles = positions[:, None] * inverse[None, :]
    cosine = jnp.concatenate([jnp.cos(angles), jnp.cos(angles)], axis=-1)[:, None, :]
    sine_part = jnp.concatenate([jnp.sin(angles), jnp.sin(angles)], axis=-1)[:, None, :]
    turned = jnp.concatenate([-key_rows[..., half_dim:], key_rows[..., :half_dim]], axis=-1)
    return key_rows * cosine + turned * sine_part


def finish(partial_value, kv_bias, offset, lengths, groups):
    span_len = partial_value.shape[1]
    biased = partial_value + kv_bias.astype(jnp.float32).reshape(2, groups, HD)
    rotated = rotary(biased[:, :, 0], offset)
    merged = jnp.stack([rotated, biased[:, :, 1]], axis=2)
    positions = jnp.arange(span_len) + offset
    live_rows = positions[None, :] < lengths[:, None]
    return jnp.where(live_rows[:, :, None, None, None], merged, 0.0).astype(jnp.bfloat16)


def folder(weight_mat):

    def add_slab(running, slab, first_col):
        col_count = slab.shape[-1]
        return jnp.dot(slab.reshape(-1, col_count), weight_mat, preferred_element_type=jnp.float32)

    return add_slab


def attend(query_rows, slot_kv, new_kv, slot_len, groups):
    slot_count = query_rows.shape[0]
    queries = query_rows.reshape(slot_count, STEPS, groups, QPK, HD)
    cached = slot_kv.reshape(slot_count, -1, 2, groups, HD)
    recent = new_kv.reshape(slot_count, STEPS, 2, groups, HD)
    score_scale = HD ** (-0.5)
    old_scores = (
        jnp.einsum(
            "rtgqd,rpgd->rtgqp", queries, cached[:, :, 0], preferred_element_type=jnp.float32
        )
        * score_scale
    )
    new_scores = (
        jnp.einsum(
            "rtgqd,rsgd->rtgqs", queries, recent[:, :, 0], preferred_element_type=jnp.float32
        )
        * score_scale
    )
    prompt_slots = cached.shape[1]
    prompt_pos = jnp.arange(prompt_slots)
    old_live = (prompt_pos[None, :] < slot_len[:, None])[:, None, None, None, :]
    step_pos = jnp.arange(STEPS)
    new_live = (step_pos[None, :] <= step_pos[:, None])[None, :, None, None, :]
    scores = jnp.concatenate(
        [jnp.where(old_live, old_scores, -jnp.inf), jnp.where(new_live, new_scores, -jnp.inf)],
        axis=-1,
    )
    attn_probs = jax.nn.softmax(scores, axis=-1).astype(jnp.bfloat16)
    attended = jnp.einsum(
        "rtgqp,rpgd->rtgqd",
        attn_probs[..., :prompt_slots],
        cached[:, :, 1],
        preferred_element_type=jnp.float32,
    )
    attended = attended + jnp.einsum(
        "rtgqs,rsgd->rtgqd",
        attn_probs[..., prompt_slots:],
        recent[:, :, 1],
        preferred_element_type=jnp.float32,
    )
    return attended.astype(jnp.bfloat16).reshape(slot_count, STEPS, groups * QPK * HD)


def per_device_general(hidden, kv_weight, kv_bias, prompt_len, owner, queries, new_kv, block_table):
    n_section = lax.axis_size("section")
    own_index = lax.axis_index("section")
    req_count = hidden.shape[0]
    prompt_max = hidden.shape[1]
    kv_width = kv_weight.shape[2]
    groups = kv_width // HD
    run_most = max(2, req_count // n_section)
    owner_grid = owner.reshape(n_section, req_count)
    local_owner = lax.dynamic_index_in_dim(owner_grid, own_index, 0, keepdims=False)
    local_len = lax.dynamic_slice_in_dim(prompt_len, own_index * req_count, req_count)
    local_ids = jnp.arange(req_count)
    earlier = (local_owner[:, None] == local_owner[None, :]) & (
        local_ids[None, :] < local_ids[:, None]
    )
    send_pos = local_owner * run_most + jnp.sum(earlier.astype(jnp.int32), axis=1)
    run_rank = jnp.cumsum((owner_grid == own_index).astype(jnp.int32), axis=1) - 1
    slot_order = jnp.argsort(owner, stable=True)
    own_slots = lax.dynamic_slice_in_dim(slot_order, own_index * req_count, req_count)
    recv_pos = own_slots // req_count * run_most + run_rank.reshape(-1)[own_slots]
    slot_len = prompt_len[own_slots]
    weight_mat = kv_weight.reshape(kv_weight.shape[0], 2 * kv_width)
    add_slab = folder(weight_mat)
    blank_acc = jnp.zeros((req_count * prompt_max, 2 * kv_width), jnp.float32)
    partial_value = add_slab(
        blank_acc, lax.all_gather(hidden, "tensor", axis=2, tiled=True), jnp.int32(0)
    )
    span_len = partial_value.shape[0] // req_count
    shaped = partial_value.reshape(req_count, span_len, 2, groups, HD)
    kv_rows = finish(shaped, kv_bias, 0, local_len, groups).reshape(
        req_count, span_len, 2, kv_width
    )
    blank_buf = jnp.zeros((n_section * run_most,) + kv_rows.shape[1:], kv_rows.dtype)
    arrived = lax.all_to_all(
        blank_buf.at[send_pos].set(kv_rows), "section", split_axis=0, concat_axis=0, tiled=True
    )
    slot_kv = jnp.take(arrived, recv_pos, axis=0)
    decode_out = attend(queries, slot_kv, new_kv, slot_len, groups)
    block_count = prompt_max // BLK
    blocks = slot_kv.reshape(req_count * block_count, BLK, 2, kv_width)
    pool_rows = jnp.zeros_like(blocks).at[block_table.reshape(-1)].set(blocks)
    return (jnp.transpose(pool_rows, (2, 0, 1, 3)), decode_out)

MESH = pl.DeviceIdType.MESH
RUNS = 4


def partner_of(me, step):
    if step == 0:
        return 3 - me
    if step == 1:
        return lax.rem(me + 2, 4)
    if step == 2:
        return me + 1 - 2 * lax.rem(me, 2)
    return me


def routed_kernel(
    head, h_ref, x0_ref, w_hbm, bias_ref, cos_ref, sin_ref, owner_ref, len_ref, inv_ref, q_ref, new_ref,
    pool_ref, out_ref,
    gathered, weight, kvbuf, sendbuf,
    w_sem, sib_send, sib_recv, x_send, x_recv, head_send, head_recv, fwd_send, fwd_recv, z_send, z_recv,
):
    sec = lax.axis_index("section")
    me = lax.axis_index("tensor")
    sib = me + 1 - 2 * lax.rem(me, 2)
    across = lax.rem(me + 2, 4)
    across_sib = lax.rem(sib + 2, 4)
    order = (me, sib, across, across_sib)
    rest = gathered.shape[3] - head

    barrier = pltpu.get_barrier_semaphore()
    pl.semaphore_signal(barrier, inc=1, device_id={"tensor": sib}, device_id_type=MESH)
    pl.semaphore_signal(barrier, inc=1, device_id={"tensor": across}, device_id_type=MESH)
    for step in range(3):
        pl.semaphore_signal(
            barrier, inc=1, device_id={"section": partner_of(sec, step)}, device_id_type=MESH
        )
    w_copies = [
        pltpu.make_async_copy(w_hbm.at[:, t], weight.at[:, t], w_sem.at[i])
        for i, t in enumerate(order)
    ]

    def run_of(source, target):
        found = jnp.int32(0)
        for r in range(1, RUNS):
            found = jnp.where(owner_ref[source * 16 + r * 4] == target, r, found)
        return found

    runs = [run_of(sec, partner_of(sec, j)) for j in range(RUNS)]

    def remote(src, dst, send, recv, where):
        return pltpu.make_async_remote_copy(
            src_ref=src, dst_ref=dst, send_sem=send, recv_sem=recv, device_id=where, device_id_type=MESH
        )

    def same(slot, send, recv, where):
        return remote(slot, slot, send, recv, where)

    cut_a, cut_b = rest // 2, rest // 3
    cuts = [
        [(0, head, cut_b), (1, head + cut_b, rest - cut_b)],
        [(2, head, rest)],
        [(3, head, rest)],
        [(4, head, cut_a), (5, head + cut_a, cut_b), (6, head + cut_a + cut_b, rest - cut_a - cut_b)],
    ]
    x_copies = [
        [
            same(
                gathered.at[j, me, :, pl.ds(first, width)],
                x_send.at[i],
                x_recv.at[i],
                {"tensor": across},
            )
            for i, first, width in cuts[j]
        ]
        for j in range(RUNS)
    ]
    pieces = [copy for copies in x_copies for copy in copies]
    sib_copies = [
        same(gathered.at[j, me], sib_send.at[j], sib_recv.at[j], {"tensor": sib}) for j in range(RUNS)
    ]
    head_copies = [
        same(
            gathered.at[j, across, :, pl.ds(0, head)], head_send.at[j], head_recv.at[j], {"tensor": sib}
        )
        for j in range(RUNS)
    ]
    fwd_copies = [
        [
            same(
                gathered.at[j, across, :, pl.ds(first, width)],
                fwd_send.at[i],
                fwd_recv.at[i],
                {"tensor": sib},
            )
            for i, first, width in cuts[j]
        ]
        for j in range(RUNS)
    ]
    gathered[0, me] = h_ref[runs[0]]
    pl.semaphore_wait(barrier, 5)
    x_copies[0][0].start()
    x_copies[0][1].start()
    gathered[1, me] = h_ref[runs[1]]
    w_copies[0].start()
    w_copies[1].start()
    sib_copies[0].start()
    gathered[0, across, :, 0:head] = x0_ref[runs[0]]
    head_copies[0].start()
    w_copies[2].start()
    w_copies[3].start()
    for j in range(1, RUNS):
        if j > 1:
            gathered[j, me] = h_ref[runs[j]]
        sib_copies[j].start()
        gathered[j, across, :, 0:head] = x0_ref[runs[j]]
        head_copies[j].start()

    def half(j, t, first=0, width=None):
        span = pl.ds(first, gathered.shape[3] if width is None else width)
        a = gathered[j, t, :, span]
        return (
            jnp.dot(a, weight[0, t, span], preferred_element_type=jnp.float32),
            jnp.dot(a, weight[1, t, span], preferred_element_type=jnp.float32),
        )

    row = lax.broadcasted_iota(jnp.int32, (128, 128), 0)
    col = lax.broadcasted_iota(jnp.int32, (128, 128), 1)
    same_slot = (row // 32) == (col // 32)
    row16 = lax.broadcasted_iota(jnp.int32, (128, 16), 0)
    col16 = lax.broadcasted_iota(jnp.int32, (128, 16), 1)
    new_live = ((row16 // 32) == (col16 // 4)) & ((col16 % 4) <= ((row16 % 32) // 8))
    contract = (((1,), (1,)), ((), ()))

    def within(index, source, run):
        first = source * 16 + run * 4
        limit = jnp.full(index.shape, len_ref[first], jnp.int32)
        for i in range(1, 4):
            limit = jnp.where(index // 32 == i, len_ref[first + i], limit)
        return (index % 32) < limit

    def attend_run(s):
        old_live = same_slot & within(col, s, run_of(s, sec))
        for g in range(2):
            q = q_ref[g, s]
            kv = kvbuf[pl.ds(8 * s, 8)].reshape(128, 512)
            k = kv[:, g * 128 : (g + 1) * 128]
            v = kv[:, 256 + g * 128 : 256 + (g + 1) * 128]
            old = lax.dot_general(q, k, contract, preferred_element_type=jnp.float32) * HD ** (-0.5)
            new = (
                lax.dot_general(q, new_ref[0, g, s], contract, preferred_element_type=jnp.float32)
                * HD ** (-0.5)
            )
            old = jnp.where(old_live, old, -jnp.inf)
            new = jnp.where(new_live, new, -jnp.inf)
            top = jnp.maximum(
                jnp.max(old, axis=1, keepdims=True), jnp.max(new, axis=1, keepdims=True)
            )
            old = jnp.exp(old - top)
            new = jnp.exp(new - top)
            total = jnp.sum(old, axis=1, keepdims=True) + jnp.sum(new, axis=1, keepdims=True)
            old = (old / total).astype(jnp.bfloat16)
            new = (new / total).astype(jnp.bfloat16)
            res = jnp.dot(old, v, preferred_element_type=jnp.float32) + jnp.dot(
                new, new_ref[1, g, s], preferred_element_type=jnp.float32
            )
            out_ref[g, s] = res.astype(jnp.bfloat16)

    bias = bias_ref[...].astype(jnp.float32)
    z_copies = []
    for j in range(RUNS):
        if j == 0:
            w_copies[0].wait()
        k_acc, v_acc = half(j, me)
        sib_copies[j].wait_recv()
        if j == 0:
            w_copies[1].wait()
        k_one, v_one = half(j, sib)
        k_acc, v_acc = k_acc + k_one, v_acc + v_one
        if j > 0:
            z_copies[j - 1].wait_recv()
            attend_run(partner_of(sec, j - 1))
        if j == 0:
            w_copies[2].wait()
            w_copies[3].wait()
        head_copies[j].wait_recv()
        for t in (across, across_sib):
            k_one, v_one = half(j, t, 0, head)
            k_acc, v_acc = k_acc + k_one, v_acc + v_one
        for at, (_, first, width) in enumerate(cuts[j]):
            x_copies[j][at].wait_recv()
            fwd_copies[j][at].start()
            if cuts[j][at][0] + 2 < len(pieces):
                pieces[cuts[j][at][0] + 2].start()
            k_one, v_one = half(j, across, first, width)
            k_acc, v_acc = k_acc + k_one, v_acc + v_one
            fwd_copies[j][at].wait_recv()
            k_one, v_one = half(j, across_sib, first, width)
            k_acc, v_acc = k_acc + k_one, v_acc + v_one
        k_acc = k_acc + bias[0:1, :]
        v_acc = v_acc + bias[1:2, :]
        live = within(row, sec, runs[j])
        parts = []
        for g in range(2):
            k = k_acc[:, g * 128 : (g + 1) * 128]
            k = k * cos_ref[...] + pltpu.roll(k, 64, 1) * sin_ref[...]
            parts.append(jnp.where(live, k, 0.0).astype(jnp.bfloat16))
        for g in range(2):
            parts.append(jnp.where(live, v_acc[:, g * 128 : (g + 1) * 128], 0.0).astype(jnp.bfloat16))
        done = jnp.concatenate(parts, axis=1).reshape(8, 16, 512)
        if j < RUNS - 1:
            sendbuf[j] = done
            copy = remote(
                sendbuf.at[j],
                kvbuf.at[pl.ds(8 * sec, 8)],
                z_send.at[j],
                z_recv.at[j],
                {"section": partner_of(sec, j)},
            )
            copy.start()
            z_copies.append(copy)
        else:
            kvbuf[pl.ds(8 * sec, 8)] = done
    attend_run(sec)
    for block in range(pool_ref.shape[1]):
        rows_in = kvbuf[inv_ref[block]]
        pool_ref[0, block] = rows_in[:, :256]
        pool_ref[1, block] = rows_in[:, 256:]
    for j in range(RUNS):
        sib_copies[j].wait_send()
        head_copies[j].wait_send()
        for at in range(len(cuts[j])):
            fwd_copies[j][at].wait_send()
            x_copies[j][at].wait_send()
        if j < RUNS - 1:
            z_copies[j].wait_send()


HEAD = 512


def per_device_routed(hidden, kv_weight, kv_bias, prompt_len, owner, queries, new_kv, block_table):
    req_count, prompt_max, feats = hidden.shape
    run = req_count // RUNS
    rows = run * prompt_max
    across = lax.ppermute(
        hidden[:, :, :HEAD].reshape(RUNS, rows, HEAD), "tensor", [(t, (t + 2) % 4) for t in range(4)]
    )
    by_run = hidden.reshape(RUNS, rows, feats)
    weight = kv_weight.reshape(4, feats, 2, 256).transpose(2, 0, 1, 3)
    positions = jnp.arange(prompt_max)
    table = block_table.reshape(-1)
    count = table.shape[0]
    inverse = jnp.sum(
        jnp.where(table[None, :] == jnp.arange(count)[:, None], jnp.arange(count)[None, :], 0), axis=1
    ).astype(jnp.int32)
    freq = rope_base ** (-(jnp.arange(HD // 2).astype(jnp.float32) * 2.0 / HD))
    angles = positions.astype(jnp.float32)[:, None] * freq[None, :]
    cosine = jnp.concatenate([jnp.cos(angles), jnp.cos(angles)], axis=-1)
    sine = jnp.concatenate([-jnp.sin(angles), jnp.sin(angles)], axis=-1)
    cosine = jnp.tile(cosine, (run, 1))
    sine = jnp.tile(sine, (run, 1))
    q = queries.reshape(4, run, STEPS, 2, QPK, HD).transpose(3, 0, 1, 2, 4, 5).reshape(2, 4, rows, HD)
    new = new_kv.reshape(4, run, STEPS, 2, 2, HD).transpose(3, 4, 0, 1, 2, 5)
    new = new.reshape(2, 2, 4, run * STEPS, HD)
    vmem = pl.BlockSpec(memory_space=pltpu.VMEM)
    smem = pl.BlockSpec(memory_space=pltpu.SMEM)
    hbm = pl.BlockSpec(memory_space=pltpu.HBM)
    dma = pltpu.SemaphoreType.DMA
    pool, out = pl.pallas_call(
        functools.partial(routed_kernel, HEAD),
        out_shape=(
            jax.ShapeDtypeStruct((2, count, BLK, 256), jnp.bfloat16),
            jax.ShapeDtypeStruct((2, 4, rows, HD), jnp.bfloat16),
        ),
        in_specs=[vmem, vmem, hbm, vmem, vmem, vmem, smem, smem, smem, vmem, vmem],
        out_specs=(vmem, vmem),
        scratch_shapes=[
            pltpu.VMEM((RUNS, 4, rows, feats), jnp.bfloat16),
            pltpu.VMEM((2, 4, feats, 256), jnp.bfloat16),
            pltpu.VMEM((count, BLK, 512), jnp.bfloat16),
            pltpu.VMEM((RUNS - 1, 8, BLK, 512), jnp.bfloat16),
        ]
        + [dma((7,))] * 11,
        compiler_params=pltpu.CompilerParams(
            collective_id=0, has_side_effects=True, vmem_limit_bytes=50 * 1024 * 1024
        ),
        cost_estimate=pl.CostEstimate(
            flops=2 * RUNS * rows * 4 * feats * 512, bytes_accessed=16 * 1024 * 1024, transcendentals=0
        ),
    )(by_run, across, weight, kv_bias, cosine, sine, owner, prompt_len, inverse, q, new)
    out = out.reshape(2, 4, run, STEPS, QPK, HD).transpose(1, 2, 3, 0, 4, 5)
    return (pool, out.reshape(req_count, STEPS, 2 * QPK * HD))


def solution(mesh):
    routed = mesh.shape["section"] == RUNS and mesh.shape["tensor"] == 4
    per_device = per_device_routed if routed else per_device_general
    return jax.shard_map(
        per_device,
        mesh=mesh,
        in_specs=(
            P(("groups", "section"), None, "tensor"),
            P(None, None, "tensor"),
            P(None, "tensor"),
            P("groups"),
            P("groups"),
            P(("groups", "section"), None, "tensor"),
            P(("groups", "section"), None, None, "tensor"),
            P(("groups", "section"), None),
        ),
        out_specs=(
            P(None, ("groups", "section"), None, "tensor"),
            P(("groups", "section"), None, "tensor"),
        ),
        check_vma=False,
    )
```

```python
import functools

import jax
import jax.numpy as jnp
from jax import lax
from jax.experimental import pallas as pl
from jax.experimental.pallas import tpu as pltpu
from jax.sharding import PartitionSpec as P

HD = 128
BLK = 16
STEPS = 4
QPK = 8


rope_base = 1000000.0


def rotary(key_rows, offset):
    half_dim = key_rows.shape[-1] // 2
    row_count = key_rows.shape[-3]
    positions = (jnp.arange(row_count) + offset).astype(jnp.float32)
    inverse = rope_base ** (-(jnp.arange(half_dim).astype(jnp.float32) * 2.0 / key_rows.shape[-1]))
    angles = positions[:, None] * inverse[None, :]
    cosine = jnp.concatenate([jnp.cos(angles), jnp.cos(angles)], axis=-1)[:, None, :]
    sine_part = jnp.concatenate([jnp.sin(angles), jnp.sin(angles)], axis=-1)[:, None, :]
    turned = jnp.concatenate([-key_rows[..., half_dim:], key_rows[..., :half_dim]], axis=-1)
    return key_rows * cosine + turned * sine_part


def finish(partial_value, kv_bias, offset, lengths, groups):
    span_len = partial_value.shape[1]
    biased = partial_value + kv_bias.astype(jnp.float32).reshape(2, groups, HD)
    rotated = rotary(biased[:, :, 0], offset)
    merged = jnp.stack([rotated, biased[:, :, 1]], axis=2)
    positions = jnp.arange(span_len) + offset
    live_rows = positions[None, :] < lengths[:, None]
    return jnp.where(live_rows[:, :, None, None, None], merged, 0.0).astype(jnp.bfloat16)


def folder(weight_mat):

    def add_slab(running, slab, first_col):
        col_count = slab.shape[-1]
        return jnp.dot(slab.reshape(-1, col_count), weight_mat, preferred_element_type=jnp.float32)

    return add_slab


def attend(query_rows, slot_kv, new_kv, slot_len, groups):
    slot_count = query_rows.shape[0]
    queries = query_rows.reshape(slot_count, STEPS, groups, QPK, HD)
    cached = slot_kv.reshape(slot_count, -1, 2, groups, HD)
    recent = new_kv.reshape(slot_count, STEPS, 2, groups, HD)
    score_scale = HD ** (-0.5)
    old_scores = (
        jnp.einsum(
            "rtgqd,rpgd->rtgqp", queries, cached[:, :, 0], preferred_element_type=jnp.float32
        )
        * score_scale
    )
    new_scores = (
        jnp.einsum(
            "rtgqd,rsgd->rtgqs", queries, recent[:, :, 0], preferred_element_type=jnp.float32
        )
        * score_scale
    )
    prompt_slots = cached.shape[1]
    prompt_pos = jnp.arange(prompt_slots)
    old_live = (prompt_pos[None, :] < slot_len[:, None])[:, None, None, None, :]
    step_pos = jnp.arange(STEPS)
    new_live = (step_pos[None, :] <= step_pos[:, None])[None, :, None, None, :]
    scores = jnp.concatenate(
        [jnp.where(old_live, old_scores, -jnp.inf), jnp.where(new_live, new_scores, -jnp.inf)],
        axis=-1,
    )
    attn_probs = jax.nn.softmax(scores, axis=-1).astype(jnp.bfloat16)
    attended = jnp.einsum(
        "rtgqp,rpgd->rtgqd",
        attn_probs[..., :prompt_slots],
        cached[:, :, 1],
        preferred_element_type=jnp.float32,
    )
    attended = attended + jnp.einsum(
        "rtgqs,rsgd->rtgqd",
        attn_probs[..., prompt_slots:],
        recent[:, :, 1],
        preferred_element_type=jnp.float32,
    )
    return attended.astype(jnp.bfloat16).reshape(slot_count, STEPS, groups * QPK * HD)


def per_device_general(hidden, kv_weight, kv_bias, prompt_len, owner, queries, new_kv, block_table):
    n_section = lax.axis_size("section")
    own_index = lax.axis_index("section")
    req_count = hidden.shape[0]
    prompt_max = hidden.shape[1]
    kv_width = kv_weight.shape[2]
    groups = kv_width // HD
    run_most = max(2, req_count // n_section)
    owner_grid = owner.reshape(n_section, req_count)
    local_owner = lax.dynamic_index_in_dim(owner_grid, own_index, 0, keepdims=False)
    local_len = lax.dynamic_slice_in_dim(prompt_len, own_index * req_count, req_count)
    local_ids = jnp.arange(req_count)
    earlier = (local_owner[:, None] == local_owner[None, :]) & (
        local_ids[None, :] < local_ids[:, None]
    )
    send_pos = local_owner * run_most + jnp.sum(earlier.astype(jnp.int32), axis=1)
    run_rank = jnp.cumsum((owner_grid == own_index).astype(jnp.int32), axis=1) - 1
    slot_order = jnp.argsort(owner, stable=True)
    own_slots = lax.dynamic_slice_in_dim(slot_order, own_index * req_count, req_count)
    recv_pos = own_slots // req_count * run_most + run_rank.reshape(-1)[own_slots]
    slot_len = prompt_len[own_slots]
    weight_mat = kv_weight.reshape(kv_weight.shape[0], 2 * kv_width)
    add_slab = folder(weight_mat)
    blank_acc = jnp.zeros((req_count * prompt_max, 2 * kv_width), jnp.float32)
    partial_value = add_slab(
        blank_acc, lax.all_gather(hidden, "tensor", axis=2, tiled=True), jnp.int32(0)
    )
    span_len = partial_value.shape[0] // req_count
    shaped = partial_value.reshape(req_count, span_len, 2, groups, HD)
    kv_rows = finish(shaped, kv_bias, 0, local_len, groups).reshape(
        req_count, span_len, 2, kv_width
    )
    blank_buf = jnp.zeros((n_section * run_most,) + kv_rows.shape[1:], kv_rows.dtype)
    arrived = lax.all_to_all(
        blank_buf.at[send_pos].set(kv_rows), "section", split_axis=0, concat_axis=0, tiled=True
    )
    slot_kv = jnp.take(arrived, recv_pos, axis=0)
    decode_out = attend(queries, slot_kv, new_kv, slot_len, groups)
    block_count = prompt_max // BLK
    blocks = slot_kv.reshape(req_count * block_count, BLK, 2, kv_width)
    pool_rows = jnp.zeros_like(blocks).at[block_table.reshape(-1)].set(blocks)
    return (jnp.transpose(pool_rows, (2, 0, 1, 3)), decode_out)

MESH = pl.DeviceIdType.MESH
RUNS = 4


def partner_of(me, step):
    if step == 0:
        return 3 - me
    if step == 1:
        return lax.rem(me + 2, 4)
    if step == 2:
        return me + 1 - 2 * lax.rem(me, 2)
    return me


def routed_kernel(
    head, h_ref, x0_ref, w_hbm, bias_ref, cos_ref, sin_ref, owner_ref, len_ref, inv_ref, q_ref, new_ref,
    pool_ref, out_ref,
    gathered, weight, kvbuf, sendbuf,
    w_sem, sib_send, sib_recv, x_send, x_recv, head_send, head_recv, fwd_send, fwd_recv, z_send, z_recv,
):
    sec = lax.axis_index("section")
    me = lax.axis_index("tensor")
    sib = me + 1 - 2 * lax.rem(me, 2)
    across = lax.rem(me + 2, 4)
    across_sib = lax.rem(sib + 2, 4)
    order = (me, sib, across, across_sib)
    rest = gathered.shape[3] - head

    barrier = pltpu.get_barrier_semaphore()
    pl.semaphore_signal(barrier, inc=1, device_id={"tensor": sib}, device_id_type=MESH)
    pl.semaphore_signal(barrier, inc=1, device_id={"tensor": across}, device_id_type=MESH)
    for step in range(3):
        pl.semaphore_signal(
            barrier, inc=1, device_id={"section": partner_of(sec, step)}, device_id_type=MESH
        )
    w_copies = [
        pltpu.make_async_copy(w_hbm.at[:, t], weight.at[:, t], w_sem.at[i])
        for i, t in enumerate(order)
    ]

    def run_of(source, target):
        found = jnp.int32(0)
        for r in range(1, RUNS):
            found = jnp.where(owner_ref[source * 16 + r * 4] == target, r, found)
        return found

    runs = [run_of(sec, partner_of(sec, j)) for j in range(RUNS)]

    def remote(src, dst, send, recv, where):
        return pltpu.make_async_remote_copy(
            src_ref=src, dst_ref=dst, send_sem=send, recv_sem=recv, device_id=where, device_id_type=MESH
        )

    def same(slot, send, recv, where):
        return remote(slot, slot, send, recv, where)

    tail = pl.ds(head, rest)
    x_copies = [
        same(gathered.at[j, me, :, tail], x_send.at[j], x_recv.at[j], {"tensor": across})
        for j in range(RUNS)
    ]
    sib_copies = [
        same(gathered.at[j, me], sib_send.at[j], sib_recv.at[j], {"tensor": sib}) for j in range(RUNS)
    ]
    head_copies = [
        same(
            gathered.at[j, across, :, pl.ds(0, head)], head_send.at[j], head_recv.at[j], {"tensor": sib}
        )
        for j in range(RUNS)
    ]
    fwd_copies = [
        same(gathered.at[j, across, :, tail], fwd_send.at[j], fwd_recv.at[j], {"tensor": sib})
        for j in range(RUNS)
    ]
    gathered[0, me] = h_ref[runs[0]]
    pl.semaphore_wait(barrier, 5)
    x_copies[0].start()
    gathered[1, me] = h_ref[runs[1]]
    x_copies[1].start()
    w_copies[0].start()
    w_copies[1].start()
    sib_copies[0].start()
    gathered[0, across, :, 0:head] = x0_ref[runs[0]]
    head_copies[0].start()
    w_copies[2].start()
    w_copies[3].start()
    for j in range(1, RUNS):
        if j > 1:
            gathered[j, me] = h_ref[runs[j]]
        sib_copies[j].start()
        gathered[j, across, :, 0:head] = x0_ref[runs[j]]
        head_copies[j].start()

    def half(j, t):
        a = gathered[j, t]
        return (
            jnp.dot(a, weight[0, t], preferred_element_type=jnp.float32),
            jnp.dot(a, weight[1, t], preferred_element_type=jnp.float32),
        )

    row = lax.broadcasted_iota(jnp.int32, (128, 128), 0)
    col = lax.broadcasted_iota(jnp.int32, (128, 128), 1)
    same_slot = (row // 32) == (col // 32)
    row16 = lax.broadcasted_iota(jnp.int32, (128, 16), 0)
    col16 = lax.broadcasted_iota(jnp.int32, (128, 16), 1)
    new_live = ((row16 // 32) == (col16 // 4)) & ((col16 % 4) <= ((row16 % 32) // 8))
    contract = (((1,), (1,)), ((), ()))

    def within(index, source, run):
        first = source * 16 + run * 4
        limit = jnp.full(index.shape, len_ref[first], jnp.int32)
        for i in range(1, 4):
            limit = jnp.where(index // 32 == i, len_ref[first + i], limit)
        return (index % 32) < limit

    def attend_run(s):
        old_live = same_slot & within(col, s, run_of(s, sec))
        for g in range(2):
            q = q_ref[g, s]
            kv = kvbuf[pl.ds(8 * s, 8)].reshape(128, 512)
            k = kv[:, g * 128 : (g + 1) * 128]
            v = kv[:, 256 + g * 128 : 256 + (g + 1) * 128]
            old = lax.dot_general(q, k, contract, preferred_element_type=jnp.float32) * HD ** (-0.5)
            new = (
                lax.dot_general(q, new_ref[0, g, s], contract, preferred_element_type=jnp.float32)
                * HD ** (-0.5)
            )
            old = jnp.where(old_live, old, -jnp.inf)
            new = jnp.where(new_live, new, -jnp.inf)
            top = jnp.maximum(
                jnp.max(old, axis=1, keepdims=True), jnp.max(new, axis=1, keepdims=True)
            )
            old = jnp.exp(old - top)
            new = jnp.exp(new - top)
            total = jnp.sum(old, axis=1, keepdims=True) + jnp.sum(new, axis=1, keepdims=True)
            old = (old / total).astype(jnp.bfloat16)
            new = (new / total).astype(jnp.bfloat16)
            res = jnp.dot(old, v, preferred_element_type=jnp.float32) + jnp.dot(
                new, new_ref[1, g, s], preferred_element_type=jnp.float32
            )
            out_ref[g, s] = res.astype(jnp.bfloat16)

    bias = bias_ref[...].astype(jnp.float32)
    z_copies = []
    for j in range(RUNS):
        if j == 0:
            w_copies[0].wait()
        k_acc, v_acc = half(j, me)
        sib_copies[j].wait_recv()
        if j == 0:
            w_copies[1].wait()
        k_one, v_one = half(j, sib)
        k_acc, v_acc = k_acc + k_one, v_acc + v_one
        if j > 0:
            z_copies[j - 1].wait_recv()
            attend_run(partner_of(sec, j - 1))
        x_copies[j].wait_recv()
        fwd_copies[j].start()
        if j + 2 < RUNS:
            x_copies[j + 2].start()
        if j == 0:
            w_copies[2].wait()
        k_one, v_one = half(j, across)
        k_acc, v_acc = k_acc + k_one, v_acc + v_one
        head_copies[j].wait_recv()
        fwd_copies[j].wait_recv()
        if j == 0:
            w_copies[3].wait()
        k_one, v_one = half(j, across_sib)
        k_acc, v_acc = k_acc + k_one, v_acc + v_one
        k_acc = k_acc + bias[0:1, :]
        v_acc = v_acc + bias[1:2, :]
        live = within(row, sec, runs[j])
        parts = []
        for g in range(2):
            k = k_acc[:, g * 128 : (g + 1) * 128]
            k = k * cos_ref[...] + pltpu.roll(k, 64, 1) * sin_ref[...]
            parts.append(jnp.where(live, k, 0.0).astype(jnp.bfloat16))
        for g in range(2):
            parts.append(jnp.where(live, v_acc[:, g * 128 : (g + 1) * 128], 0.0).astype(jnp.bfloat16))
        done = jnp.concatenate(parts, axis=1).reshape(8, 16, 512)
        if j < RUNS - 1:
            sendbuf[j] = done
            copy = remote(
                sendbuf.at[j],
                kvbuf.at[pl.ds(8 * sec, 8)],
                z_send.at[j],
                z_recv.at[j],
                {"section": partner_of(sec, j)},
            )
            copy.start()
            z_copies.append(copy)
        else:
            kvbuf[pl.ds(8 * sec, 8)] = done
    attend_run(sec)
    for block in range(pool_ref.shape[1]):
        rows_in = kvbuf[inv_ref[block]]
        pool_ref[0, block] = rows_in[:, :256]
        pool_ref[1, block] = rows_in[:, 256:]
    for j in range(RUNS):
        sib_copies[j].wait_send()
        head_copies[j].wait_send()
        fwd_copies[j].wait_send()
        x_copies[j].wait_send()
        if j < RUNS - 1:
            z_copies[j].wait_send()


HEAD = 512


def per_device_routed(hidden, kv_weight, kv_bias, prompt_len, owner, queries, new_kv, block_table):
    req_count, prompt_max, feats = hidden.shape
    run = req_count // RUNS
    rows = run * prompt_max
    across = lax.ppermute(
        hidden[:, :, :HEAD].reshape(RUNS, rows, HEAD), "tensor", [(t, (t + 2) % 4) for t in range(4)]
    )
    by_run = hidden.reshape(RUNS, rows, feats)
    weight = kv_weight.reshape(4, feats, 2, 256).transpose(2, 0, 1, 3)
    positions = jnp.arange(prompt_max)
    table = block_table.reshape(-1)
    count = table.shape[0]
    inverse = jnp.sum(
        jnp.where(table[None, :] == jnp.arange(count)[:, None], jnp.arange(count)[None, :], 0), axis=1
    ).astype(jnp.int32)
    freq = rope_base ** (-(jnp.arange(HD // 2).astype(jnp.float32) * 2.0 / HD))
    angles = positions.astype(jnp.float32)[:, None] * freq[None, :]
    cosine = jnp.concatenate([jnp.cos(angles), jnp.cos(angles)], axis=-1)
    sine = jnp.concatenate([-jnp.sin(angles), jnp.sin(angles)], axis=-1)
    cosine = jnp.tile(cosine, (run, 1))
    sine = jnp.tile(sine, (run, 1))
    q = queries.reshape(4, run, STEPS, 2, QPK, HD).transpose(3, 0, 1, 2, 4, 5).reshape(2, 4, rows, HD)
    new = new_kv.reshape(4, run, STEPS, 2, 2, HD).transpose(3, 4, 0, 1, 2, 5)
    new = new.reshape(2, 2, 4, run * STEPS, HD)
    vmem = pl.BlockSpec(memory_space=pltpu.VMEM)
    smem = pl.BlockSpec(memory_space=pltpu.SMEM)
    hbm = pl.BlockSpec(memory_space=pltpu.HBM)
    dma = pltpu.SemaphoreType.DMA
    pool, out = pl.pallas_call(
        functools.partial(routed_kernel, HEAD),
        out_shape=(
            jax.ShapeDtypeStruct((2, count, BLK, 256), jnp.bfloat16),
            jax.ShapeDtypeStruct((2, 4, rows, HD), jnp.bfloat16),
        ),
        in_specs=[vmem, vmem, hbm, vmem, vmem, vmem, smem, smem, smem, vmem, vmem],
        out_specs=(vmem, vmem),
        scratch_shapes=[
            pltpu.VMEM((RUNS, 4, rows, feats), jnp.bfloat16),
            pltpu.VMEM((2, 4, feats, 256), jnp.bfloat16),
            pltpu.VMEM((count, BLK, 512), jnp.bfloat16),
            pltpu.VMEM((RUNS - 1, 8, BLK, 512), jnp.bfloat16),
        ]
        + [dma((4,))] * 11,
        compiler_params=pltpu.CompilerParams(
            collective_id=0, has_side_effects=True, vmem_limit_bytes=50 * 1024 * 1024
        ),
        cost_estimate=pl.CostEstimate(
            flops=2 * RUNS * rows * 4 * feats * 512, bytes_accessed=16 * 1024 * 1024, transcendentals=0
        ),
    )(by_run, across, weight, kv_bias, cosine, sine, owner, prompt_len, inverse, q, new)
    out = out.reshape(2, 4, run, STEPS, QPK, HD).transpose(1, 2, 3, 0, 4, 5)
    return (pool, out.reshape(req_count, STEPS, 2 * QPK * HD))


def solution(mesh):
    routed = mesh.shape["section"] == RUNS and mesh.shape["tensor"] == 4
    per_device = per_device_routed if routed else per_device_general
    return jax.shard_map(
        per_device,
        mesh=mesh,
        in_specs=(
            P(("groups", "section"), None, "tensor"),
            P(None, None, "tensor"),
            P(None, "tensor"),
            P("groups"),
            P("groups"),
            P(("groups", "section"), None, "tensor"),
            P(("groups", "section"), None, None, "tensor"),
            P(("groups", "section"), None),
        ),
        out_specs=(
            P(None, ("groups", "section"), None, "tensor"),
            P(("groups", "section"), None, "tensor"),
        ),
        check_vma=False,
    )
```
